32 devices in a mesh: grp: 2 (over y), seq: 4 (over z), mdl: 4 (over x, core).
Axes of the slice: x: 2, y: 2, z: 4, core: 2. Of those that a mesh axis runs over, the one named last changes fastest.
Arguments:
- class_rows: bfloat16 [2048, 1536], P(('grp', 'seq')), parts along dimension 0, may hold values from -6 to 6
- destination: int32 [2048, 1], P(('grp', 'seq')), parts along dimension 0, may hold values from 0 to 3; in each aligned block of 256 rows (0 to 255, 256 to 511, ...) at most 128 rows name the same one
- norm1_gain: float32 [1536], replicated, may hold values from 0.5 to 1.5
- gate_weight: bfloat16 [1536, 4096], P(None, 'mdl'), may hold values from -0.15625 to 0.15625
- up_weight: bfloat16 [1536, 4096], P(None, 'mdl'), may hold values from -0.15625 to 0.15625
- down_weight: bfloat16 [4096, 1536], P('mdl'), may hold values from -0.09375 to 0.09375
- layer_scale: float32 [1536], replicated, may hold values from 0.3 to 1.5
- norm2_gain: float32 [1536], replicated, may hold values from 0.5 to 1.5
- proj_weight: bfloat16 [1536, 768], P(None, 'mdl'), may hold values from -0.15625 to 0.15625
- norm3_gain: float32 [768], replicated, may hold values from 0.5 to 1.5
- query_weight: bfloat16 [768, 768], P(None, 'mdl'), may hold values from -1 to 1
- key_weight: bfloat16 [768, 768], P(None, 'mdl'), may hold values from -1 to 1
- value_weight: bfloat16 [768, 768], P(None, 'mdl'), may hold values from -0.21875 to 0.21875
- out_weight: bfloat16 [768, 768], P('mdl'), may hold values from -0.21875 to 0.21875
Outputs:
- slide_out: bfloat16 [4096, 768], P(('grp', 'seq'), 'mdl'), parts along dimension 0
The draws below stay inside these ranges and needn't reach their ends.
There are 2 independent parts, one for each index of `grp`. The reference program is written for one: setup_inputs(seed, part) draws one part's arguments, and reference() takes and returns one part's arrays. A program takes and returns all parts, laid end to end along the dimension named above; an argument that names none is the same for every part. Nothing has to cross between parts.
Inputs may be any that keep to these rules, and one draw needn't show every extreme that they name: `destination`: among the rows of one device each owner is named by at most 128 rows, and by exactly 128 in some device's rows; every owner is named by some row.
All inputs are finite; a program needn't handle non-finite values.
Results may differ from the reference program's by a relative error of at most 0.019.
Values may be sent and summed in bfloat16 or wider, within the bound.
No kernel may reach another device: no remote copies, remote signals or barrier semaphores. Data moves between devices by JAX's collectives and lax.ppermute only.
A program may use at most 128 MiB of HBM per device.

```python
import math
import jax
import jax.numpy as jnp
import numpy as np
from jax import lax

E = 1536
FF = 4096
D = 768
HEADS = 16
HD = 48
TILE_DEV = 256
RATE = 4
CAP = 128
SLOT_DEV = 512
SEQLEN = 2048
TILES = 1024
N_SEQ = 4


def drawn_part(key):
    sign_key = jax.random.fold_in(key, 101)
    column_key = jax.random.fold_in(key, 102)
    order_key = jax.random.fold_in(key, 103)
    signs = jax.random.rademacher(sign_key, (D,), jnp.float32) * D ** (-0.5)
    direction = jnp.clip(jax.random.normal(column_key, (D,), jnp.float32), -3.0, 3.0)
    ladder = jnp.arange(HEADS, dtype=jnp.float32) / max(HEADS - 1, 1)
    strength = 0.3 * jnp.exp(ladder * jnp.log(2.5 / 0.3))
    order = jax.random.permutation(order_key, HEADS)
    head_strength = strength[order]
    head_of = jnp.arange(D, dtype=jnp.int32) // HD
    amplitude = head_strength[head_of]
    return signs[:, None] * (direction * amplitude)[None, :]


def noise_part(key):
    noise = jnp.clip(jax.random.normal(key, (D, D), jnp.float32), -4.0, 4.0)
    return noise * D ** (-0.5)


def draw_query_weight(key, part):
    aligned = drawn_part(key)
    key = jax.random.fold_in(key, 7)
    return jnp.clip(aligned + noise_part(key), -1.0, 1.0).astype(jnp.bfloat16)


def draw_key_weight(key, part):
    aligned = drawn_part(key)
    key = jax.random.fold_in(key, 11)
    return jnp.clip(aligned + noise_part(key), -1.0, 1.0).astype(jnp.bfloat16)


def steps_of(rng, dims, split, least, top_value):
    level, own = 1.0, jax.random.fold_in(rng, 6)
    for axis_at, shards_of in split:
        heights = jnp.exp(jax.random.uniform(jax.random.fold_in(own, axis_at), (shards_of,), jnp.float32, least / len(split), top_value / len(split)))
        level = level * jnp.repeat(heights, dims[axis_at] // shards_of).reshape([-1 if axis == axis_at else 1 for axis in range(len(dims))])
    return level


def assign_block(rng, own, number, rows, count, top, limit, skew):
    order = jax.random.permutation(rng, count)
    crowded, ordinary = shares(count, rows * top, limit, skew, True), shares(count, rows * top, limit, skew, False)
    places = jnp.arange(count)

    def named(lengths, turn):
        used = int((lengths > 0).sum())
        fixed = max(1, used // 4)
        passed = fixed + (places - fixed + turn * (used - fixed)) % max(1, count - fixed)
        return jnp.zeros((count,), jnp.int32).at[order[jnp.where(places < fixed, places, passed)]].set(jnp.asarray(lengths, jnp.int32))

    lengths = jnp.where(number % 4 == 0, named(crowded, number // 4), named(ordinary, number - number // 4 - 1))
    mixed = jax.random.permutation(jax.random.fold_in(own, 3), count)
    source_of, receiver = mixed[0:count // 2 * 2:2], mixed[1:count // 2 * 2:2]
    room = jnp.minimum(lengths[source_of] - 1, limit - lengths[receiver]) // 2
    room = jnp.where((source_of == order[0]) | (receiver == order[0]) | (lengths[receiver] == 0), 0, jnp.maximum(room, 0))
    passed = jax.random.randint(jax.random.fold_in(own, 4), (count // 2,), 0, 1 << 20) % (room + 1)
    lengths = lengths.at[source_of].add(-passed).at[receiver].add(passed)
    members = jnp.searchsorted(jnp.cumsum(lengths), jnp.arange(rows * top), side="right").astype(jnp.int32)
    grid = members.reshape(top, rows).T
    grid = grid[jax.random.permutation(jax.random.fold_in(own, 1), rows)]
    turn = jax.random.randint(jax.random.fold_in(own, 2), (rows, 1), 0, top)
    return jnp.take_along_axis(grid, (jnp.arange(top)[None, :] + turn) % top, axis=1)


def shares(number_of, total, limit, lean, full):
    portions = [(1 << 20) // math.isqrt(rank ** lean) + 1 for rank in range(1, number_of + 1)]
    largest = limit if full else min(limit, max(-(-total // number_of), total * portions[0] // sum(portions)))
    least = 1 if total - largest >= number_of - 1 else 0
    counts, surplus = [largest] + [least] * (number_of - 1), total - largest - least * (number_of - 1)
    while surplus > 0:
        free = [i for i in range(1, number_of) if counts[i] < largest] or [i for i in range(1, number_of) if counts[i] < limit]
        whole, remaining = sum([portions[i] for i in free]), surplus
        for i in free:
            addition = min(limit - counts[i], max(1, remaining * portions[i] // whole), surplus)
            counts[i] = counts[i] + addition
            surplus = surplus - addition
    return np.array(counts)


def normal_values(own_key, dims, width, limit, split=(), kind=jnp.bfloat16):
    gain = steps_of(own_key, dims, split, -0.22, 0.18) if split else 1.0
    values = jax.random.normal(own_key, dims, jnp.float32) * width * gain
    return jnp.minimum(jnp.maximum(values, -limit), limit).astype(kind)


def setup_inputs(seed: int = 0, part: int = 0) -> dict:
    streams_of = jax.random.split(jax.random.key(seed), 15)
    part_keys = jax.random.split(jax.random.fold_in(streams_of[14], part), 15)
    class_rows = normal_values(part_keys[0], (TILES, E), 1.0, 6.0, ((0, 4),))
    destination_keys = jax.random.split(jax.random.fold_in(part_keys[1], 1), TILES // TILE_DEV)
    destination_turns = jax.random.permutation(jax.random.fold_in(part_keys[1], 3), TILES // TILE_DEV)
    destination = jax.vmap(lambda own, number: assign_block(jax.random.fold_in(part_keys[1], 2), own, number, TILE_DEV, N_SEQ, 1, CAP, 2))(destination_keys, destination_turns).reshape((TILES, 1))
    norm1_gain = jnp.clip(1.0 + 0.1 * jax.random.normal(streams_of[2], (E,), jnp.float32), 0.5, 1.5)
    gate_weight = normal_values(streams_of[3], (E, FF), E ** -0.5, 0.15625, ((1, 4),))
    up_weight = normal_values(streams_of[4], (E, FF), E ** -0.5, 0.15625, ((1, 4),))
    down_weight = normal_values(streams_of[5], (FF, E), FF ** -0.5, 0.09375, ((0, 4),))
    layer_scale = jnp.clip(jnp.exp(jax.random.uniform(streams_of[6], (E,), jnp.float32, math.log(0.3), math.log(1.5))), 0.3, 1.5)
    norm2_gain = jnp.clip(1.0 + 0.1 * jax.random.normal(streams_of[7], (E,), jnp.float32), 0.5, 1.5)
    proj_weight = normal_values(streams_of[8], (E, D), E ** -0.5, 0.15625, ((1, 4),))
    norm3_gain = jnp.clip(1.0 + 0.1 * jax.random.normal(streams_of[9], (D,), jnp.float32), 0.5, 1.5)
    query_weight = draw_query_weight(jax.random.fold_in(streams_of[14], 71), part)
    key_weight = draw_key_weight(jax.random.fold_in(streams_of[14], 71), part)
    value_weight = normal_values(streams_of[12], (D, D), D ** -0.5, 0.21875, ((1, 4),))
    out_weight = normal_values(streams_of[13], (D, D), D ** -0.5, 0.21875, ((0, 4),))
    return {"class_rows": class_rows, "destination": destination, "norm1_gain": norm1_gain, "gate_weight": gate_weight, "up_weight": up_weight, "down_weight": down_weight, "layer_scale": layer_scale, "norm2_gain": norm2_gain, "proj_weight": proj_weight, "norm3_gain": norm3_gain, "query_weight": query_weight, "key_weight": key_weight, "value_weight": value_weight, "out_weight": out_weight}


epsilon = 1e-06
masked_score = -1e+30

def layer_norm(features, norm_gain):
    middle = lax.optimization_barrier(jnp.mean(features, axis=-1, keepdims=True))
    centred = features - middle
    spread = lax.optimization_barrier(jnp.mean(centred * centred, axis=-1, keepdims=True))
    return centred * lax.rsqrt(spread + epsilon) * norm_gain

def encode(class_rows, norm1_gain, gate_weight, up_weight, down_weight, layer_scale, norm2_gain, proj_weight):
    normed = layer_norm(class_rows.astype(jnp.float32), norm1_gain.astype(jnp.float32)).astype(jnp.bfloat16)
    gate = jnp.dot(normed, gate_weight, preferred_element_type=jnp.float32)
    upward = jnp.dot(normed, up_weight, preferred_element_type=jnp.float32)
    hidden = (jax.nn.silu(gate) * upward).astype(jnp.bfloat16)
    feedfwd = jnp.dot(hidden, down_weight, preferred_element_type=jnp.float32)
    stream = class_rows.astype(jnp.float32) + layer_scale.astype(jnp.float32) * feedfwd
    final = layer_norm(stream, norm2_gain.astype(jnp.float32)).astype(jnp.bfloat16)
    return jnp.dot(final, proj_weight, preferred_element_type=jnp.float32).astype(jnp.bfloat16)

def attend_set(queries, keys, values, live_keys):
    scale = HD ** (-0.5)
    scores = jnp.einsum('qhd,khd->hqk', queries.astype(jnp.float32), keys.astype(jnp.float32)) * scale
    alive = live_keys[None, None, :] > 0
    scores = jnp.where(alive, scores, masked_score)
    peak = lax.optimization_barrier(jnp.max(scores, axis=-1))
    weights = jnp.where(alive, jnp.exp(scores - peak[..., None]), 0.0)
    total = lax.optimization_barrier(jnp.sum(weights, axis=-1))
    rounded = lax.optimization_barrier(weights.astype(jnp.bfloat16)).astype(jnp.float32)
    summed = jnp.einsum('hqk,khd->qhd', rounded, values.astype(jnp.float32))
    return (peak.T, total.T, summed)

def reference(class_rows, destination, norm1_gain, gate_weight, up_weight, down_weight, layer_scale, norm2_gain, proj_weight, norm3_gain, query_weight, key_weight, value_weight, out_weight):
    embedded = encode(class_rows, norm1_gain, gate_weight, up_weight, down_weight, layer_scale, norm2_gain, proj_weight)
    target = destination[:, 0].astype(jnp.int32)
    onehot = (target[:, None] == jnp.arange(N_SEQ, dtype=jnp.int32)[None, :]).astype(jnp.int32)
    blocked = onehot.reshape(N_SEQ, TILE_DEV, N_SEQ)
    earlier = jnp.cumsum(blocked, axis=1) - blocked
    arrival = lax.optimization_barrier(jnp.sum(earlier * blocked, axis=2)).reshape(TILES).astype(jnp.int32)
    source = jnp.arange(TILES, dtype=jnp.int32) // TILE_DEV
    position = (target * SLOT_DEV + source * CAP + arrival).astype(jnp.int32)
    sequence = jnp.zeros((SEQLEN, D), jnp.bfloat16).at[position].set(embedded)
    occupied = jnp.zeros((SEQLEN,), jnp.float32).at[position].set(1.0)
    normed = layer_norm(sequence.astype(jnp.float32), norm3_gain.astype(jnp.float32)).astype(jnp.bfloat16)
    queries = jnp.dot(normed, query_weight, preferred_element_type=jnp.float32).astype(jnp.bfloat16).reshape(SEQLEN, HEADS, HD)
    keys = jnp.dot(normed, key_weight, preferred_element_type=jnp.float32).astype(jnp.bfloat16).reshape(SEQLEN, HEADS, HD)
    values = jnp.dot(normed, value_weight, preferred_element_type=jnp.float32).astype(jnp.bfloat16).reshape(SEQLEN, HEADS, HD)

    def local_segment(segment):
        return attend_set(segment[0], segment[1], segment[2], segment[3])
    peak_local, total_local, summed_local = lax.map(local_segment, (queries.reshape(N_SEQ, SLOT_DEV, HEADS, HD), keys.reshape(N_SEQ, SLOT_DEV, HEADS, HD), values.reshape(N_SEQ, SLOT_DEV, HEADS, HD), occupied.reshape(N_SEQ, SLOT_DEV)))
    peak_local = peak_local.reshape(SEQLEN, HEADS)
    total_local = total_local.reshape(SEQLEN, HEADS)
    summed_local = summed_local.reshape(SEQLEN, HEADS, HD)
    sparse_all = SEQLEN // RATE
    peak_list = []
    total_list = []
    summed_list = []
    for head in range(HEADS):
        picked = (jnp.arange(sparse_all, dtype=jnp.int32) * RATE + head % RATE).astype(jnp.int32)
        peak_one, total_one, summed_one = attend_set(queries[picked, head][:, None, :], keys[picked, head][:, None, :], values[picked, head][:, None, :], occupied[picked])
        peak_list.append(jnp.full((SEQLEN,), masked_score, jnp.float32).at[picked].set(peak_one[:, 0]))
        total_list.append(jnp.zeros((SEQLEN,), jnp.float32).at[picked].set(total_one[:, 0]))
        summed_list.append(jnp.zeros((SEQLEN, HD), jnp.float32).at[picked].set(summed_one[:, 0, :]))
    peak_sparse = jnp.stack(peak_list, axis=1)
    total_sparse = jnp.stack(total_list, axis=1)
    summed_sparse = jnp.stack(summed_list, axis=1)
    highest = jnp.maximum(peak_local, peak_sparse)
    first_weight = jnp.exp(peak_local - highest)
    second_weight = jnp.exp(peak_sparse - highest)
    mixed = (first_weight[..., None] * summed_local + second_weight[..., None] * summed_sparse) / (first_weight * total_local + second_weight * total_sparse)[..., None]
    attended = mixed.reshape(SEQLEN, D).astype(jnp.bfloat16)
    projected = jnp.dot(attended, out_weight, preferred_element_type=jnp.float32)
    return ((sequence.astype(jnp.float32) + projected) * occupied[:, None]).astype(jnp.bfloat16)
```

```python
import functools

import jax
import jax.numpy as jnp
from jax import lax
from jax.experimental import pallas as pl
from jax.experimental.pallas import tpu as pltpu
from jax.sharding import PartitionSpec as P

HD = 48
RATE = 4
EPSILON = 1e-06
MASKED = -1e30
VMEM_LIMIT = 48 * 1024 * 1024
LOG2E = 1.4426950408889634

f32 = jnp.float32
bf16 = jnp.bfloat16


def layer_norm(features, norm_gain):
    middle = jnp.mean(features, axis=-1, keepdims=True)
    centred = features - middle
    spread = jnp.mean(centred * centred, axis=-1, keepdims=True)
    return centred * lax.rsqrt(spread + EPSILON) * norm_gain


def dot(a, b):
    return jnp.dot(a, b, preferred_element_type=f32)


def dot_t(a, b):
    return lax.dot_general(a, b, (((1,), (1,)), ((), ())), preferred_element_type=f32)


def whole(shape):
    return pl.BlockSpec(shape, lambda *_: (0,) * len(shape))


SMEM = pl.BlockSpec(memory_space=pltpu.SMEM)
VMEM = pl.BlockSpec(memory_space=pltpu.VMEM)


def ffn_kernel(where_ref, rows_ref, gain_ref, gate_ref, up_ref, down_ref, keep_ref, send_ref, normed, total):
    step = pl.program_id(0)
    me = where_ref[0]
    share = rows_ref.shape[0] // 4

    @pl.when(step == 0)
    def _():
        for place, other in enumerate((0, 2, 1, 3)):
            start = pl.multiple_of((me ^ other) * share, share)
            rows = rows_ref[pl.ds(start, share), :].astype(f32)
            normed[place * share : (place + 1) * share, :] = layer_norm(rows, gain_ref[...]).astype(bf16)

    gate = dot(normed[...], gate_ref[...])
    upward = dot(normed[...], up_ref[...])
    hidden = (gate * jax.nn.sigmoid(gate) * upward).astype(bf16)
    part = dot(hidden, down_ref[...])

    @pl.when(step == 0)
    def _():
        total[...] = part

    @pl.when(step > 0)
    def _():
        total[...] += part

    @pl.when(step == pl.num_programs(0) - 1)
    def _():
        keep_ref[...] = total[: 2 * share, :]
        send_ref[...] = total[2 * share :, :].astype(bf16)


def feed_forward(where, rows, gain, gate_weight, up_weight, down_weight):
    tiles, width = rows.shape
    hidden = gate_weight.shape[1]
    steps = 4
    chunk = hidden // steps
    half = tiles // 2
    return pl.pallas_call(
        ffn_kernel,
        grid=(steps,),
        in_specs=[
            SMEM,
            whole((tiles, width)),
            whole((1, width)),
            pl.BlockSpec((width, chunk), lambda i: (0, i)),
            pl.BlockSpec((width, chunk), lambda i: (0, i)),
            pl.BlockSpec((chunk, width), lambda i: (i, 0)),
        ],
        out_specs=[whole((half, width)), whole((half, width))],
        out_shape=[jax.ShapeDtypeStruct((half, width), f32), jax.ShapeDtypeStruct((half, width), bf16)],
        scratch_shapes=[pltpu.VMEM((tiles, width), bf16), pltpu.VMEM((tiles, width), f32)],
        compiler_params=pltpu.CompilerParams(vmem_limit_bytes=VMEM_LIMIT),
        cost_estimate=pl.CostEstimate(
            flops=6 * tiles * width * hidden, bytes_accessed=6 * width * hidden, transcendentals=tiles * hidden
        ),
        name="feed_forward",
    )(where, rows, gain, gate_weight, up_weight, down_weight)


def embed_kernel(
    where_ref, rows_ref, keep_ref, near_ref, far_ref, scale_ref, gain_ref, p0, p1, p2, p3, out_ref, blocks
):
    me = where_ref[0]
    share = out_ref.shape[0]
    start = pl.multiple_of(me * share, share)
    rows = rows_ref[pl.ds(start, share), :].astype(f32)
    feedfwd = keep_ref[...] + near_ref[...].astype(f32) + far_ref[...].astype(f32)
    stream = rows + scale_ref[...] * feedfwd
    final = layer_norm(stream, gain_ref[...]).astype(bf16)
    for other, weight in enumerate((p0, p1, p2, p3)):
        blocks[me ^ other] = dot(final, weight[...])
    out_ref[...] = jnp.concatenate([blocks[k] for k in range(4)], axis=1).astype(bf16)


def embed(where, rows, keep, near, far, scale, gain, pieces):
    tiles, width = rows.shape
    share = far.shape[0]
    columns = pieces[0].shape[1]
    first = pl.BlockSpec((share, width), lambda i: (0, 0))
    return pl.pallas_call(
        embed_kernel,
        grid=(1,),
        in_specs=[SMEM, whole((tiles, width)), first, first, whole((share, width)), whole((1, width)), whole((1, width))]
        + [whole((width, columns))] * 4,
        out_specs=whole((share, 4 * columns)),
        out_shape=jax.ShapeDtypeStruct((share, 4 * columns), bf16),
        scratch_shapes=[pltpu.VMEM((4, share, columns), f32)],
        compiler_params=pltpu.CompilerParams(vmem_limit_bytes=VMEM_LIMIT),
        cost_estimate=pl.CostEstimate(
            flops=8 * share * width * columns, bytes_accessed=8 * width * columns, transcendentals=0
        ),
        name="embed",
    )(where, rows, keep, near, far, scale, gain, *pieces)


def loop(count, body):
    if count <= 4:
        for i in range(count):
            body(i)
    else:
        pl.loop(0, count)(body)


def attend_kernel(n, piece_count, *refs):
    where_ref = refs[0]
    pieces = refs[1 : 1 + piece_count]
    owners = refs[1 + piece_count : 1 + 2 * piece_count] if piece_count == 1 else refs[1 + piece_count : 1 + piece_count + n]
    rest = refs[1 + piece_count + len(owners) :]
    gain_ref, wq, wk, wv, att_ref, res_ref = rest[:6]
    emb, named, kall, vall, qloc, kloc, vloc, occ, cls = rest[6:15]
    scores_sc = rest[15]
    me, here = where_ref[0], where_ref[1]
    tiles = emb.shape[1]
    cap = qloc.shape[1]
    columns = wq.shape[1]
    width = emb.shape[2]
    heads = columns // HD
    slots = n * cap

    if piece_count == 1:
        source, named_of = pieces[0], owners[0]
    else:
        source, named_of = emb, named
        share = tiles // 4
        for kz in range(n):
            named[here ^ kz] = owners[kz][...]
            for km in range(4):
                at = pl.multiple_of((me ^ km) * share, share)
                emb[here ^ kz, pl.ds(at, share), :] = pieces[kz * 4 + km][...]

    earlier_of = lax.broadcasted_iota(jnp.int32, (tiles, tiles), 0) < lax.broadcasted_iota(
        jnp.int32, (tiles, tiles), 1
    )
    before = jnp.where(earlier_of, 1.0, 0.0).astype(bf16)
    mine = (
        lax.broadcasted_iota(jnp.int32, (width, columns), 0)
        == lax.broadcasted_iota(jnp.int32, (width, columns), 1) + me * columns
    )
    pick_columns = jnp.where(mine, 1.0, 0.0).astype(bf16)
    n_pad = max(n, 8)
    owner_ids = lax.broadcasted_iota(jnp.int32, (n_pad, tiles), 0)
    slot_ids = lax.broadcasted_iota(jnp.int32, (cap, tiles), 0)

    def block(b):
        owner = named_of[b]
        onehot = jnp.where(owner_ids == owner, 1.0, 0.0)
        earlier = dot(onehot.astype(bf16), before)
        arrival = jnp.sum(onehot * earlier, axis=0, keepdims=True).astype(jnp.int32)
        cls[b] = arrival & (RATE - 1)
        chosen = jnp.where((slot_ids == arrival) & (owner == here), 1.0, 0.0)
        occ[b] = jnp.broadcast_to(jnp.sum(chosen, axis=1, keepdims=True), (cap, 128)).astype(bf16)
        chosen = chosen.astype(bf16)
        rows = source[b]
        res_ref[b] = dot(chosen, dot(rows, pick_columns).astype(bf16)).astype(bf16)
        normed = layer_norm(rows.astype(f32), gain_ref[...]).astype(bf16)
        queries = dot(normed, wq[...]).astype(bf16)
        keys = dot(normed, wk[...]).astype(bf16)
        values = dot(normed, wv[...]).astype(bf16)
        kall[b] = keys
        vall[b] = values
        qloc[b] = dot(chosen, queries).astype(bf16)
        kloc[b] = dot(chosen, keys).astype(bf16)
        vloc[b] = dot(chosen, values).astype(bf16)

    loop(n, block)

    factor = HD ** (-0.5) * LOG2E
    key_local = kloc[...].reshape(slots, columns)
    value_local = vloc[...].reshape(slots, columns)
    live = dot_t(jnp.full((8, 128), 1.0, bf16), occ[...].reshape(slots, 128))[0:1, :]
    bias_local = jnp.where(live > 0.5, 0.0, MASKED)
    chunk = slots // 4
    per = min(n, 4)
    parts = n // per
    span = per * tiles
    head_of = lax.broadcasted_iota(jnp.int32, (chunk, columns), 1) // HD
    row_class = lax.broadcasted_iota(jnp.int32, (chunk, 1), 0) & (RATE - 1)
    blocks_per = max(n // 4, 1)

    for c in range(4):
        if n >= 4:
            q = qloc[c * blocks_per : (c + 1) * blocks_per].reshape(chunk, columns)
            occupied = occ[c * blocks_per : (c + 1) * blocks_per].reshape(chunk, 128)[:, 0:1]
        else:
            q = qloc[...].reshape(slots, columns)[c * chunk : (c + 1) * chunk]
            occupied = occ[...].reshape(slots, 128)[c * chunk : (c + 1) * chunk, 0:1]
        picked = jnp.where(head_of == row_class, q, jnp.zeros((), bf16))

        def classes(s):
            return jnp.concatenate([cls[s * per + i] for i in range(per)], axis=1)

        if parts == 1:
            keys = kall[...].reshape(span, columns)
            sparse = jnp.where(row_class == classes(0), dot_t(picked, keys) * factor, MASKED)
            peak_sparse = jnp.max(sparse, axis=1, keepdims=True)
            weights = jnp.exp2(sparse - peak_sparse)
            total_sparse = jnp.sum(weights, axis=1, keepdims=True)
            summed_sparse = dot(weights.astype(bf16), vall[...].reshape(span, columns))
        else:

            def first(s, peak):
                keys = kall[pl.ds(s * per, per)].reshape(span, columns)
                sparse = jnp.where(row_class == classes(s), dot_t(picked, keys) * factor, MASKED)
                scores_sc[s] = sparse
                return jnp.maximum(peak, jnp.max(sparse, axis=1, keepdims=True))

            peak_sparse = lax.fori_loop(0, parts, first, jnp.full((chunk, 1), MASKED, f32))

            def second(s, carry):
                total, summed = carry
                weights = jnp.exp2(scores_sc[s] - peak_sparse)
                values = vall[pl.ds(s * per, per)].reshape(span, columns)
                return (
                    total + jnp.sum(weights, axis=1, keepdims=True),
                    summed + dot(weights.astype(bf16), values),
                )

            total_sparse, summed_sparse = lax.fori_loop(
                0, parts, second, (jnp.zeros((chunk, 1), f32), jnp.zeros((chunk, columns), f32))
            )

        mixed = jnp.zeros((chunk, columns), f32)
        for h in range(heads):
            query = jnp.where(head_of == h, q, jnp.zeros((), bf16))
            scores = dot_t(query, key_local) * factor + bias_local
            peak = jnp.max(scores, axis=1, keepdims=True)
            weights = jnp.exp2(scores - peak)
            total = jnp.sum(weights, axis=1, keepdims=True)
            summed = dot(weights.astype(bf16), value_local)
            has = row_class == (h % RATE)
            highest = jnp.where(has, jnp.maximum(peak, peak_sparse), peak)
            first_weight = jnp.exp2(peak - highest)
            second_weight = jnp.where(has, jnp.exp2(peak_sparse - highest), 0.0)
            share_of = 1.0 / (first_weight * total + second_weight * total_sparse)
            both = (first_weight * share_of) * summed + (second_weight * share_of) * summed_sparse
            mixed = jnp.where(head_of == h, both, mixed)
        att_ref[c * chunk : (c + 1) * chunk, :] = jnp.where(occupied > 0.5, mixed, 0.0).astype(bf16)


def attend(where, pieces, owners, gain, wq, wk, wv, n, tiles):
    width, columns = wq.shape
    slots = 2 * tiles
    cap = slots // n
    per = min(n, 4)
    parts = n // per
    loose = len(pieces) > 1
    args = [where, *pieces, *owners, gain, wq, wk, wv]
    return pl.pallas_call(
        functools.partial(attend_kernel, n, len(pieces)),
        in_specs=[SMEM] + [VMEM] * (len(args) - 1),
        out_specs=[VMEM, VMEM],
        out_shape=[jax.ShapeDtypeStruct((slots, columns), bf16), jax.ShapeDtypeStruct((n, cap, columns), bf16)],
        scratch_shapes=[
            pltpu.VMEM((n if loose else 1, tiles, width), bf16),
            pltpu.VMEM((n if loose else 1, 1, tiles), jnp.int32),
            pltpu.VMEM((n, tiles, columns), bf16),
            pltpu.VMEM((n, tiles, columns), bf16),
            pltpu.VMEM((n, cap, columns), bf16),
            pltpu.VMEM((n, cap, columns), bf16),
            pltpu.VMEM((n, cap, columns), bf16),
            pltpu.VMEM((n, cap, 128), bf16),
            pltpu.VMEM((n, 1, tiles), jnp.int32),
            pltpu.VMEM((parts if parts > 1 else 1, slots // 4 if parts > 1 else 8, per * tiles), f32),
        ],
        compiler_params=pltpu.CompilerParams(vmem_limit_bytes=VMEM_LIMIT),
        cost_estimate=pl.CostEstimate(
            flops=2 * n * tiles * width * columns * 3, bytes_accessed=2 * n * tiles * width, transcendentals=slots * slots * 4
        ),
        name="attend",
    )(*args)


def output_kernel(a0, a1, a2, a3, w0, w1, w2, w3, res_ref, out_ref):
    total = dot(a0[...], w0[...]) + dot(a1[...], w1[...]) + dot(a2[...], w2[...]) + dot(a3[...], w3[...])
    out_ref[...] = (total + res_ref[...].astype(f32)).astype(bf16)


def project_out(attended, weights, residual):
    return pl.pallas_call(
        output_kernel,
        in_specs=[VMEM] * 9,
        out_specs=VMEM,
        out_shape=jax.ShapeDtypeStruct(residual.shape, bf16),
        compiler_params=pltpu.CompilerParams(vmem_limit_bytes=VMEM_LIMIT),
        name="project_out",
    )(*attended, *weights, residual)


def per_device(
    class_rows,
    destination,
    norm1_gain,
    gate_weight,
    up_weight,
    down_weight,
    layer_scale,
    norm2_gain,
    proj_weight,
    norm3_gain,
    query_weight,
    key_weight,
    value_weight,
    out_weight,
):
    tiles = class_rows.shape[0]
    n = lax.axis_size("seq")
    me = lax.axis_index("mdl")
    here = lax.axis_index("seq")
    where = jnp.stack([me, here]).astype(jnp.int32)
    columns = query_weight.shape[1]
    share = tiles // 4

    def over_mdl(value, k):
        return lax.ppermute(value, "mdl", [(i, i ^ k) for i in range(4)])

    def over_seq(value, k):
        return lax.ppermute(value, "seq", [(i, i ^ k) for i in range(n)])

    proj_far = over_mdl(proj_weight, 2)
    proj_near = over_mdl(proj_weight, 1)
    proj_cross = over_mdl(proj_far, 1)

    owner = destination.reshape(1, tiles)
    few = n <= 4
    if few:
        owners = [owner] + [over_seq(owner, k) for k in range(1, n)]
    else:
        owners = [lax.all_gather(owner, "seq", axis=0)]

    keep, send = feed_forward(
        where, class_rows, norm1_gain[None], gate_weight, up_weight, down_weight
    )
    near = over_mdl(send, 1)
    onward = (keep[share:] + near[share:].astype(f32)).astype(bf16)
    far = over_mdl(onward, 2)
    embedded = embed(
        where,
        class_rows,
        keep,
        near,
        far,
        layer_scale[None],
        norm2_gain[None],
        (proj_weight, proj_near, proj_far, proj_cross),
    )
    if few:
        pieces = []
        for k in range(n):
            own = over_seq(embedded, k) if k else embedded
            across = over_mdl(own, 2)
            pieces += [own, over_mdl(own, 1), across, over_mdl(across, 1)]
    else:
        gathered = lax.all_gather(lax.all_gather(embedded, "mdl", axis=0, tiled=True), "seq", axis=0)
        pieces = [gathered]
    attended, residual = attend(
        where, pieces, owners, norm3_gain[None], query_weight, key_weight, value_weight, n, tiles
    )
    residual = residual.reshape(attended.shape)

    def out_block(k):
        return lax.dynamic_slice_in_dim(out_weight, (me ^ k) * columns, columns, axis=1)

    out_blocks = [out_block(0)] + [over_mdl(out_block(k), k) for k in (1, 2, 3)]
    beyond = over_mdl(attended, 2)
    gathered = [attended, over_mdl(attended, 1), beyond, over_mdl(beyond, 1)]
    return project_out(gathered, out_blocks, residual)


def solution(mesh):
    return jax.shard_map(
        per_device,
        mesh=mesh,
        in_specs=(
            P(("grp", "seq"), None),
            P(("grp", "seq"), None),
            P(),
            P(None, "mdl"),
            P(None, "mdl"),
            P("mdl", None),
            P(),
            P(),
            P(None, "mdl"),
            P(),
            P(None, "mdl"),
            P(None, "mdl"),
            P(None, "mdl"),
            P("mdl", None),
        ),
        out_specs=P(("grp", "seq"), "mdl"),
        check_vma=False,
    )
```

```python
import functools

import jax
import jax.numpy as jnp
from jax import lax
from jax.experimental import pallas as pl
from jax.experimental.pallas import tpu as pltpu
from jax.sharding import PartitionSpec as P

HD = 48
RATE = 4
EPSILON = 1e-06
MASKED = -1e30
MIB = 1024 * 1024
LOG2E = 1.4426950408889634

f32 = jnp.float32
bf16 = jnp.bfloat16


def layer_norm(features, norm_gain):
    middle = jnp.mean(features, axis=-1, keepdims=True)
    centred = features - middle
    spread = jnp.mean(centred * centred, axis=-1, keepdims=True)
    return centred * lax.rsqrt(spread + EPSILON) * norm_gain


def dot(a, b):
    return jnp.dot(a, b, preferred_element_type=f32)


def dot_t(a, b):
    return lax.dot_general(a, b, (((1,), (1,)), ((), ())), preferred_element_type=f32)


def whole(shape):
    return pl.BlockSpec(shape, lambda *_: (0,) * len(shape))


VMEM = pl.BlockSpec(memory_space=pltpu.VMEM)


def mdl_index():
    return lax.axis_index("mdl")


def seq_index():
    return lax.axis_index("seq")


def row(ref):
    return ref[...].reshape(1, ref.shape[0])


def ffn_kernel(steps, rows_ref, gain_ref, gate_ref, up_ref, down_ref, keep_ref, send_ref, normed, hidden):
    step = pl.program_id(0)
    me = mdl_index()
    share = rows_ref.shape[0] // 4
    chunk = gate_ref.shape[1]

    @pl.when(step == 0)
    def _():
        for place, other in enumerate((0, 2, 1, 3)):
            start = pl.multiple_of((me ^ other) * share, share)
            rows = rows_ref[pl.ds(start, share), :].astype(f32)
            normed[place * share : (place + 1) * share, :] = layer_norm(rows, row(gain_ref)).astype(bf16)

    for i in range(steps):

        @pl.when(step == i)
        def _(i=i):
            gate = dot(normed[...], gate_ref[...])
            upward = dot(normed[...], up_ref[...])
            hidden[:, i * chunk : (i + 1) * chunk] = (gate * jax.nn.sigmoid(gate) * upward).astype(bf16)

    @pl.when(step >= steps)
    def _():
        total = dot(hidden[...], down_ref[...])
        keep_ref[...] = total[: 2 * share, :]
        send_ref[...] = total[2 * share :, :].astype(bf16)


def feed_forward(rows, gain, gate_weight, up_weight, down_weight):
    tiles, width = rows.shape
    hidden = gate_weight.shape[1]
    steps, later = 4, 4
    chunk = hidden // steps
    part = width // later
    half = tiles // 2

    def early(i):
        return (0, jnp.minimum(i, steps - 1))

    def late(i):
        return (0, jnp.maximum(i - steps, 0))

    return pl.pallas_call(
        functools.partial(ffn_kernel, steps),
        grid=(steps + later,),
        in_specs=[
            whole((tiles, width)),
            whole((width,)),
            pl.BlockSpec((width, chunk), early),
            pl.BlockSpec((width, chunk), early),
            pl.BlockSpec((hidden, part), late),
        ],
        out_specs=[pl.BlockSpec((half, part), late), pl.BlockSpec((half, part), late)],
        out_shape=[jax.ShapeDtypeStruct((half, width), f32), jax.ShapeDtypeStruct((half, width), bf16)],
        scratch_shapes=[pltpu.VMEM((tiles, width), bf16), pltpu.VMEM((tiles, hidden), bf16)],
        compiler_params=pltpu.CompilerParams(vmem_limit_bytes=60 * MIB),
        cost_estimate=pl.CostEstimate(
            flops=6 * tiles * width * hidden, bytes_accessed=6 * width * hidden, transcendentals=tiles * hidden
        ),
        name="feed_forward",
    )(rows, gain, gate_weight, up_weight, down_weight)


def embed_kernel(rows_ref, keep_ref, near_ref, far_ref, scale_ref, gain_ref, p0, p1, p2, p3, out_ref, blocks):
    me = mdl_index()
    share = out_ref.shape[0]
    start = pl.multiple_of(me * share, share)
    rows = rows_ref[pl.ds(start, share), :].astype(f32)
    feedfwd = keep_ref[...] + near_ref[...].astype(f32) + far_ref[...].astype(f32)
    stream = rows + row(scale_ref) * feedfwd
    final = layer_norm(stream, row(gain_ref)).astype(bf16)
    for other, weight in enumerate((p0, p1, p2, p3)):
        blocks[me ^ other] = dot_t(final, weight[...])
    out_ref[...] = jnp.concatenate([blocks[k] for k in range(4)], axis=1).astype(bf16)


def embed(rows, keep, near, far, scale, gain, pieces):
    tiles, width = rows.shape
    share = far.shape[0]
    columns = pieces[0].shape[0]
    first = pl.BlockSpec((share, width), lambda i: (0, 0))
    return pl.pallas_call(
        embed_kernel,
        grid=(1,),
        in_specs=[whole((tiles, width)), first, first, whole((share, width)), whole((width,)), whole((width,))]
        + [whole((columns, width))] * 4,
        out_specs=whole((share, 4 * columns)),
        out_shape=jax.ShapeDtypeStruct((share, 4 * columns), bf16),
        scratch_shapes=[pltpu.VMEM((4, share, columns), f32)],
        compiler_params=pltpu.CompilerParams(vmem_limit_bytes=16 * MIB),
        cost_estimate=pl.CostEstimate(
            flops=8 * share * width * columns, bytes_accessed=8 * width * columns, transcendentals=0
        ),
        name="embed",
    )(rows, keep, near, far, scale, gain, *pieces)


LANES = 256


def prepare_kernel(loose, *refs):
    pieces = refs[:loose]
    owner_ref, gain_ref, wq, wk, wv, local_ref, all_ref, class_ref, residual_ref, block = refs[loose:]
    me, here = mdl_index(), seq_index()
    tiles, width = block.shape
    columns = wq.shape[0]
    cap = local_ref.shape[0]
    if loose > 1:
        share = tiles // 4
        for km in range(4):
            at = pl.multiple_of((me ^ km) * share, share)
            block[pl.ds(at, share), :] = pieces[km][...]
        rows = block[...]
    else:
        rows = pieces[0][...]
    owner = owner_ref[...]
    count = max(8, 2 * tiles // cap)
    onehot = jnp.where(lax.broadcasted_iota(jnp.int32, (count, tiles), 0) == owner, 1.0, 0.0)
    earlier_of = lax.broadcasted_iota(jnp.int32, (tiles, tiles), 0) < lax.broadcasted_iota(
        jnp.int32, (tiles, tiles), 1
    )
    earlier = dot(onehot.astype(bf16), jnp.where(earlier_of, 1.0, 0.0).astype(bf16))
    arrival = jnp.sum(onehot * earlier, axis=0, keepdims=True).astype(jnp.int32)
    class_ref[...] = arrival & (RATE - 1)
    slot_ids = lax.broadcasted_iota(jnp.int32, (cap, tiles), 0)
    chosen = jnp.where((slot_ids == arrival) & (owner == here), 1.0, 0.0)
    occupied = jnp.sum(chosen, axis=1, keepdims=True)
    chosen = chosen.astype(bf16)
    mine = (
        lax.broadcasted_iota(jnp.int32, (columns, width), 1)
        == lax.broadcasted_iota(jnp.int32, (columns, width), 0) + me * columns
    )
    picked = jnp.where(mine, 1.0, 0.0).astype(bf16)
    residual_ref[...] = dot_t(dot_t(picked, rows).astype(bf16), chosen).astype(bf16)
    normed = layer_norm(rows.astype(f32), row(gain_ref)).astype(bf16)
    queries = dot_t(normed, wq[...]).astype(bf16)
    keys = dot_t(normed, wk[...]).astype(bf16)
    values = dot_t(normed, wv[...]).astype(bf16)
    all_ref[:, :columns] = keys
    all_ref[:, LANES : LANES + columns] = values
    local_ref[:, :columns] = dot(chosen, queries).astype(bf16)
    local_ref[:, columns:LANES] = jnp.broadcast_to(occupied, (cap, LANES - columns)).astype(bf16)
    local_ref[:, LANES : LANES + columns] = dot(chosen, keys).astype(bf16)
    local_ref[:, 2 * LANES : 2 * LANES + columns] = dot(chosen, values).astype(bf16)


def prepare(pieces, owner, gain, weights, cap):
    columns, width = weights[0].shape
    loose = len(pieces)
    if loose > 1:
        count, tiles = 1, owner.shape[1]
        first = [whole(pieces[0].shape)] * loose + [whole((1, tiles))]
        lead, block = (), whole
    else:
        count, _, tiles = owner.shape
        lead = (count,)

        def block(shape):
            return pl.BlockSpec((None, *shape), lambda b: (b, 0, 0))

        first = [block((tiles, width)), block((1, tiles))]
    outs = [((cap, 3 * LANES), bf16), ((tiles, 2 * LANES), bf16), ((1, tiles), jnp.int32), ((columns, cap), bf16)]
    return pl.pallas_call(
        functools.partial(prepare_kernel, loose),
        grid=(count,),
        in_specs=first + [whole((width,))] + [whole((columns, width))] * 3,
        out_specs=[block(shape) for shape, _ in outs],
        out_shape=[jax.ShapeDtypeStruct(lead + shape, kind) for shape, kind in outs],
        scratch_shapes=[pltpu.VMEM((tiles, width), bf16)],
        compiler_params=pltpu.CompilerParams(vmem_limit_bytes=16 * MIB),
        cost_estimate=pl.CostEstimate(
            flops=6 * count * tiles * width * columns, bytes_accessed=6 * width * columns, transcendentals=0
        ),
        name="prepare",
    )(*pieces, owner, gain, *weights)


def attend_kernel(n, groups, columns, *refs):
    local = refs[:groups]
    every = refs[groups : 2 * groups]
    classes = refs[2 * groups : 3 * groups]
    att_ref, scores_sc = refs[3 * groups :]
    heads = columns // HD
    slots = att_ref.shape[1]
    factor = HD ** (-0.5) * LOG2E

    def taken(start, size):
        parts = [ref[..., start : start + size] for ref in local]
        parts = [part.reshape(-1, size) for part in parts]
        return parts[0] if groups == 1 else jnp.concatenate(parts, axis=0)

    q = taken(0, columns)
    key_local = taken(LANES, columns)
    value_local = taken(2 * LANES, columns)
    flags = taken(LANES - 128, 128)
    last = jnp.where(lax.broadcasted_iota(jnp.int32, (8, 128), 1) == 127, 1.0, 0.0).astype(bf16)
    live = dot_t(last, flags)[0:1, :]
    occupied = flags[:, 127:128]
    bias_local = jnp.where(live > 0.5, 0.0, MASKED)
    head_of = lax.broadcasted_iota(jnp.int32, (slots, columns), 1) // HD
    row_class = lax.broadcasted_iota(jnp.int32, (slots, 1), 0) & (RATE - 1)
    picked = jnp.where((head_of & (RATE - 1)) == row_class, q, jnp.zeros((), bf16))

    if groups > 1 or n == 1:
        class_row = jnp.concatenate([ref[...].reshape(1, -1) for ref in classes], axis=1)
        keys = jnp.concatenate([ref[..., :columns].reshape(-1, columns) for ref in every], axis=0)
        values = jnp.concatenate([ref[..., LANES : LANES + columns].reshape(-1, columns) for ref in every], axis=0)
        sparse = jnp.where(row_class == class_row, dot_t(picked, keys) * factor, MASKED)
        peak_sparse = jnp.max(sparse, axis=1, keepdims=True)
        weights = jnp.exp2(sparse - peak_sparse)
        total_sparse = jnp.sum(weights, axis=1, keepdims=True)
        summed_sparse = dot(weights.astype(bf16), values)
    else:

        def first(b, peak):
            keys = every[0][b, :, :columns]
            sparse = jnp.where(row_class == classes[0][b], dot_t(picked, keys) * factor, MASKED)
            scores_sc[b] = sparse
            return jnp.maximum(peak, jnp.max(sparse, axis=1, keepdims=True))

        peak_sparse = lax.fori_loop(0, n, first, jnp.full((slots, 1), MASKED, f32))

        def second(b, carry):
            total, summed = carry
            weights = jnp.exp2(scores_sc[b] - peak_sparse)
            values = every[0][b, :, LANES : LANES + columns]
            return total + jnp.sum(weights, axis=1, keepdims=True), summed + dot(weights.astype(bf16), values)

        total_sparse, summed_sparse = lax.fori_loop(
            0, n, second, (jnp.zeros((slots, 1), f32), jnp.zeros((slots, columns), f32))
        )

    mixed = jnp.zeros((slots, columns), f32)
    for h in range(heads):
        query = jnp.where(head_of == h, q, jnp.zeros((), bf16))
        scores = dot_t(query, key_local) * factor + bias_local
        peak = jnp.max(scores, axis=1, keepdims=True)
        weights = jnp.exp2(scores - peak)
        total = jnp.sum(weights, axis=1, keepdims=True)
        summed = dot(weights.astype(bf16), value_local)
        has = row_class == (h & (RATE - 1))
        highest = jnp.where(has, jnp.maximum(peak, peak_sparse), peak)
        first_weight = jnp.exp2(peak - highest)
        second_weight = jnp.where(has, jnp.exp2(peak_sparse - highest), 0.0)
        share_of = 1.0 / (first_weight * total + second_weight * total_sparse)
        both = (first_weight * share_of) * summed + (second_weight * share_of) * summed_sparse
        mixed = jnp.where(head_of == h, both, mixed)
    att_ref[...] = jnp.where(occupied > 0.5, mixed, 0.0).T.astype(bf16)


def attend(local, every, classes, n, slots, columns):
    groups = len(local)
    tiles = every[0].shape[-2]
    stored = (n, slots, tiles) if groups == 1 and n > 1 else (1, 8, 128)
    return pl.pallas_call(
        functools.partial(attend_kernel, n, groups, columns),
        in_specs=[VMEM] * (3 * groups),
        out_specs=VMEM,
        out_shape=jax.ShapeDtypeStruct((columns, slots), bf16),
        scratch_shapes=[pltpu.VMEM(stored, f32)],
        compiler_params=pltpu.CompilerParams(vmem_limit_bytes=(24 if n <= 4 else 48) * MIB),
        cost_estimate=pl.CostEstimate(
            flops=4 * slots * columns * (4 * slots + n * tiles),
            bytes_accessed=2 * n * tiles * columns,
            transcendentals=slots * (4 * slots + n * tiles),
        ),
        name="attend",
    )(*local, *every, *classes)


def output_kernel(groups, a0, a1, a2, a3, w0, w1, w2, w3, *refs):
    residual, out_ref = refs[:groups], refs[groups]
    here = seq_index()
    total = None
    for weight, piece in ((w0, a0), (w1, a1), (w2, a2), (w3, a3)):
        part = lax.dot_general(weight[...], piece[...], (((0,), (0,)), ((), ())), preferred_element_type=f32)
        total = part if total is None else total + part
    if groups == 1:
        out_ref[...] = (total + residual[0][...].astype(f32)).astype(bf16)
    else:
        cap = residual[0].shape[1]
        for k in range(groups):
            at = pl.multiple_of((here ^ k) * cap, cap)
            block = total[:, k * cap : (k + 1) * cap] + residual[k][...].astype(f32)
            out_ref[:, pl.ds(at, cap)] = block.astype(bf16)


def project_out(attended, weights, residual):
    return pl.pallas_call(
        functools.partial(output_kernel, len(residual)),
        in_specs=[VMEM] * (8 + len(residual)),
        out_specs=VMEM,
        out_shape=jax.ShapeDtypeStruct((weights[0].shape[1], attended[0].shape[1]), bf16),
        compiler_params=pltpu.CompilerParams(vmem_limit_bytes=16 * MIB),
        name="project_out",
    )(*attended, *weights, *residual)


def per_device(
    class_rows,
    destination,
    norm1_gain,
    gate_weight,
    up_weight,
    down_weight,
    layer_scale,
    norm2_gain,
    proj_weight,
    norm3_gain,
    query_weight,
    key_weight,
    value_weight,
    out_weight,
):
    tiles = class_rows.shape[0]
    n = lax.axis_size("seq")
    me = lax.axis_index("mdl")
    columns = query_weight.shape[1]
    share = tiles // 4
    slots = 2 * tiles
    cap = slots // n
    few = n <= 4

    def over_mdl(value, k):
        return lax.ppermute(value, "mdl", [(i, i ^ k) for i in range(4)])

    def over_seq(value, k):
        return lax.ppermute(value, "seq", [(i, i ^ k) for i in range(n)])

    proj = proj_weight.T
    proj_far = over_mdl(proj, 2)
    proj_near = over_mdl(proj, 1)
    proj_cross = over_mdl(proj_far, 1)

    owner = destination.reshape(1, tiles)
    if few:
        owners = [owner] + [over_seq(owner, k) for k in range(1, n)]
    else:
        owners = [lax.all_gather(owner, "seq", axis=0)]

    keep, send = feed_forward(class_rows, norm1_gain, gate_weight, up_weight, down_weight)
    near = over_mdl(send, 1)
    onward = (keep[share:] + near[share:].astype(f32)).astype(bf16)
    far = over_mdl(onward, 2)
    embedded = embed(
        class_rows, keep, near, far, layer_scale, norm2_gain, (proj, proj_near, proj_far, proj_cross)
    )

    out_late, _ = lax.optimization_barrier((out_weight, embedded))

    def out_block(k):
        return lax.dynamic_slice_in_dim(out_late, (me ^ k) * columns, columns, axis=1)

    out_blocks = [out_block(0)] + [over_mdl(out_block(k), k) for k in (1, 2, 3)]

    weights = (query_weight.T, key_weight.T, value_weight.T)
    if few:
        ready = []
        for k in range(n):
            own = over_seq(embedded, k) if k else embedded
            across = over_mdl(own, 2)
            pieces = [own, over_mdl(own, 1), across, over_mdl(across, 1)]
            ready.append(prepare(pieces, owners[k], norm3_gain, weights, cap))
    else:
        gathered = lax.all_gather(lax.all_gather(embedded, "mdl", axis=0, tiled=True), "seq", axis=0)
        ready = [prepare([gathered], owners[0], norm3_gain, weights, cap)]
    local, every, classes, residual = (list(items) for items in zip(*ready))
    local, out_blocks = lax.optimization_barrier((local, out_blocks))
    attended = attend(local, every, classes, n, slots, columns)
    if not few:
        residual = [residual[0].transpose(1, 0, 2).reshape(columns, slots)]

    beyond = over_mdl(attended, 2)
    gathered = [attended, over_mdl(attended, 1), beyond, over_mdl(beyond, 1)]
    return project_out(gathered, out_blocks, residual).T


def solution(mesh):
    return jax.shard_map(
        per_device,
        mesh=mesh,
        in_specs=(
            P(("grp", "seq"), None),
            P(("grp", "seq"), None),
            P(),
            P(None, "mdl"),
            P(None, "mdl"),
            P("mdl", None),
            P(),
            P(),
            P(None, "mdl"),
            P(),
            P(None, "mdl"),
            P(None, "mdl"),
            P(None, "mdl"),
            P("mdl", None),
        ),
        out_specs=P(("grp", "seq"), "mdl"),
        check_vma=False,
    )
```

```python
import functools

import jax
import jax.numpy as jnp
from jax import lax
from jax.experimental import pallas as pl
from jax.experimental.pallas import tpu as pltpu
from jax.sharding import PartitionSpec as P

HD = 48
RATE = 4
EPSILON = 1e-06
MASKED = -1e30
MIB = 1024 * 1024
LOG2E = 1.4426950408889634

f32 = jnp.float32
bf16 = jnp.bfloat16


def layer_norm(features, norm_gain):
    middle = jnp.mean(features, axis=-1, keepdims=True)
    centred = features - middle
    spread = jnp.mean(centred * centred, axis=-1, keepdims=True)
    return centred * lax.rsqrt(spread + EPSILON) * norm_gain


def dot(a, b):
    return jnp.dot(a, b, preferred_element_type=f32)


def dot_t(a, b):
    return lax.dot_general(a, b, (((1,), (1,)), ((), ())), preferred_element_type=f32)


def whole(shape):
    return pl.BlockSpec(shape, lambda *_: (0,) * len(shape))


VMEM = pl.BlockSpec(memory_space=pltpu.VMEM)


def mdl_index():
    return lax.axis_index("mdl")


def seq_index():
    return lax.axis_index("seq")


def row(ref):
    return ref[...].reshape(1, ref.shape[0])


def ffn_kernel(
    rows_ref, gain_ref, gate_ref, up_ref, down_ref, keep_ref, send_ref,
    rows, gate, upward, down, normed, hidden, sems,
):
    me = mdl_index()
    half = keep_ref.shape[0]
    pairs = ((rows_ref, rows), (gate_ref, gate), (up_ref, upward), (down_ref, down))
    copies = [pltpu.make_async_copy(source, target, sems.at[i]) for i, (source, target) in enumerate(pairs)]
    for copy in copies:
        copy.start()
    copies[0].wait()
    for place in range(2):
        start = pl.multiple_of(((me & 1) ^ place) * half, half)
        part = rows[pl.ds(start, half), :].astype(f32)
        normed[place * half : (place + 1) * half, :] = layer_norm(part, row(gain_ref)).astype(bf16)
    copies[1].wait()
    opened = dot(normed[...], gate[...])
    opened = opened * jax.nn.sigmoid(opened)
    copies[2].wait()
    hidden[...] = (opened * dot(normed[...], upward[...])).astype(bf16)
    copies[3].wait()
    send_ref[...] = dot(hidden[half:, :], down[...]).astype(bf16)
    keep_ref[...] = dot(hidden[:half, :], down[...])


def feed_forward(rows, gain, gate_weight, up_weight, down_weight):
    tiles, width = rows.shape
    hidden = gate_weight.shape[1]
    half = tiles // 2
    far = pl.BlockSpec(memory_space=pltpu.HBM)
    return pl.pallas_call(
        ffn_kernel,
        in_specs=[far, VMEM, far, far, far],
        out_specs=[VMEM, VMEM],
        out_shape=[jax.ShapeDtypeStruct((half, width), f32), jax.ShapeDtypeStruct((half, width), bf16)],
        scratch_shapes=[
            pltpu.VMEM((tiles, width), bf16),
            pltpu.VMEM((width, hidden), bf16),
            pltpu.VMEM((width, hidden), bf16),
            pltpu.VMEM((hidden, width), bf16),
            pltpu.VMEM((tiles, width), bf16),
            pltpu.VMEM((tiles, hidden), bf16),
            pltpu.SemaphoreType.DMA((4,)),
        ],
        compiler_params=pltpu.CompilerParams(vmem_limit_bytes=60 * MIB),
        cost_estimate=pl.CostEstimate(
            flops=6 * tiles * width * hidden, bytes_accessed=6 * width * hidden, transcendentals=tiles * hidden
        ),
        name="feed_forward",
    )(rows, gain, gate_weight, up_weight, down_weight)


def embed_kernel(rows_ref, here_ref, far_ref, scale_ref, gain_ref, own, near, out_ref, blocks):
    core = mdl_index() & 1
    half = here_ref.shape[0]
    start = pl.multiple_of(core * half, half)
    rows = rows_ref[pl.ds(start, half), :].astype(f32)
    feedfwd = here_ref[...].astype(f32) + far_ref[...].astype(f32)
    stream = rows + row(scale_ref) * feedfwd
    final = layer_norm(stream, row(gain_ref)).astype(bf16)
    blocks[core] = dot_t(final, own[...])
    blocks[core ^ 1] = dot_t(final, near[...])
    out_ref[...] = jnp.concatenate([blocks[0], blocks[1]], axis=1).astype(bf16)


def embed(rows, here, far, scale, gain, own, near):
    half, width = here.shape
    columns = own.shape[0]
    return pl.pallas_call(
        embed_kernel,
        in_specs=[VMEM] * 7,
        out_specs=VMEM,
        out_shape=jax.ShapeDtypeStruct((half, 2 * columns), bf16),
        scratch_shapes=[pltpu.VMEM((2, half, columns), f32)],
        compiler_params=pltpu.CompilerParams(vmem_limit_bytes=16 * MIB),
        cost_estimate=pl.CostEstimate(
            flops=4 * half * width * columns, bytes_accessed=4 * width * columns, transcendentals=0
        ),
        name="embed",
    )(rows, here, far, scale, gain, own, near)


LANES = 256


def prepare_kernel(loose, *refs):
    pieces = refs[:loose]
    owner_ref, gain_ref, wq, wk, wv, local_ref, all_ref, class_ref, residual_ref, block = refs[loose:]
    me, here = mdl_index(), seq_index()
    tiles, width = block.shape
    columns = wq.shape[0]
    cap = local_ref.shape[0]
    if loose > 1:
        half, side = tiles // 2, width // 2
        for km in range(4):
            at = pl.multiple_of(((me ^ km) & 1) * half, half)
            over = pl.multiple_of(((me ^ km) >> 1) * side, side)
            block[pl.ds(at, half), pl.ds(over, side)] = pieces[km][...]
        rows = block[...]
    else:
        rows = pieces[0][...]
    owner = owner_ref[...]
    count = max(8, 2 * tiles // cap)
    onehot = jnp.where(lax.broadcasted_iota(jnp.int32, (count, tiles), 0) == owner, 1.0, 0.0)
    earlier_of = lax.broadcasted_iota(jnp.int32, (tiles, tiles), 0) < lax.broadcasted_iota(
        jnp.int32, (tiles, tiles), 1
    )
    earlier = dot(onehot.astype(bf16), jnp.where(earlier_of, 1.0, 0.0).astype(bf16))
    arrival = jnp.sum(onehot * earlier, axis=0, keepdims=True).astype(jnp.int32)
    class_ref[...] = arrival & (RATE - 1)
    slot_ids = lax.broadcasted_iota(jnp.int32, (cap, tiles), 0)
    chosen = jnp.where((slot_ids == arrival) & (owner == here), 1.0, 0.0)
    occupied = jnp.sum(chosen, axis=1, keepdims=True)
    chosen = chosen.astype(bf16)
    mine = (
        lax.broadcasted_iota(jnp.int32, (columns, width), 1)
        == lax.broadcasted_iota(jnp.int32, (columns, width), 0) + me * columns
    )
    picked = jnp.where(mine, 1.0, 0.0).astype(bf16)
    residual_ref[...] = dot_t(dot_t(picked, rows).astype(bf16), chosen).astype(bf16)
    normed = layer_norm(rows.astype(f32), row(gain_ref)).astype(bf16)
    queries = dot_t(normed, wq[...]).astype(bf16)
    keys = dot_t(normed, wk[...]).astype(bf16)
    values = dot_t(normed, wv[...]).astype(bf16)
    all_ref[:, :columns] = keys
    all_ref[:, LANES : LANES + columns] = values
    local_ref[:, :columns] = dot(chosen, queries).astype(bf16)
    local_ref[:, columns:LANES] = jnp.broadcast_to(occupied, (cap, LANES - columns)).astype(bf16)
    local_ref[:, LANES : LANES + columns] = dot(chosen, keys).astype(bf16)
    local_ref[:, 2 * LANES : 2 * LANES + columns] = dot(chosen, values).astype(bf16)


def prepare(pieces, owner, gain, weights, cap):
    columns, width = weights[0].shape
    loose = len(pieces)
    if loose > 1:
        count, tiles = 1, owner.shape[1]
        first = [whole(pieces[0].shape)] * loose + [whole((1, tiles))]
        lead, block = (), whole
    else:
        count, _, tiles = owner.shape
        lead = (count,)

        def block(shape):
            return pl.BlockSpec((None, *shape), lambda b: (b, 0, 0))

        first = [block((tiles, width)), block((1, tiles))]
    outs = [((cap, 3 * LANES), bf16), ((tiles, 2 * LANES), bf16), ((1, tiles), jnp.int32), ((columns, cap), bf16)]
    return pl.pallas_call(
        functools.partial(prepare_kernel, loose),
        grid=(count,),
        in_specs=first + [whole((width,))] + [whole((columns, width))] * 3,
        out_specs=[block(shape) for shape, _ in outs],
        out_shape=[jax.ShapeDtypeStruct(lead + shape, kind) for shape, kind in outs],
        scratch_shapes=[pltpu.VMEM((tiles, width), bf16)],
        compiler_params=pltpu.CompilerParams(vmem_limit_bytes=16 * MIB),
        cost_estimate=pl.CostEstimate(
            flops=6 * count * tiles * width * columns, bytes_accessed=6 * width * columns, transcendentals=0
        ),
        name="prepare",
    )(*pieces, owner, gain, *weights)


def attend_kernel(n, groups, columns, *refs):
    local = refs[:groups]
    every = refs[groups : 2 * groups]
    classes = refs[2 * groups : 3 * groups]
    att_ref, scores_sc = refs[3 * groups :]
    heads = columns // HD
    slots = att_ref.shape[1]
    factor = HD ** (-0.5) * LOG2E

    def taken(start, size):
        parts = [ref[..., start : start + size] for ref in local]
        parts = [part.reshape(-1, size) for part in parts]
        return parts[0] if groups == 1 else jnp.concatenate(parts, axis=0)

    q = taken(0, columns)
    key_local = taken(LANES, columns)
    value_local = taken(2 * LANES, columns)
    flags = taken(LANES - 128, 128)
    last = jnp.where(lax.broadcasted_iota(jnp.int32, (8, 128), 1) == 127, 1.0, 0.0).astype(bf16)
    live = dot_t(last, flags)[0:1, :]
    occupied = flags[:, 127:128]
    bias_local = jnp.where(live > 0.5, 0.0, MASKED)
    head_of = lax.broadcasted_iota(jnp.int32, (slots, columns), 1) // HD
    row_class = lax.broadcasted_iota(jnp.int32, (slots, 1), 0) & (RATE - 1)
    picked = jnp.where((head_of & (RATE - 1)) == row_class, q, jnp.zeros((), bf16))

    if groups > 1 or n == 1:
        class_row = jnp.concatenate([ref[...].reshape(1, -1) for ref in classes], axis=1)
        keys = jnp.concatenate([ref[..., :columns].reshape(-1, columns) for ref in every], axis=0)
        values = jnp.concatenate([ref[..., LANES : LANES + columns].reshape(-1, columns) for ref in every], axis=0)
        sparse = jnp.where(row_class == class_row, dot_t(picked, keys) * factor, MASKED)
        peak_sparse = jnp.max(sparse, axis=1, keepdims=True)
        weights = jnp.exp2(sparse - peak_sparse)
        total_sparse = jnp.sum(weights, axis=1, keepdims=True)
        summed_sparse = dot(weights.astype(bf16), values)
    else:

        def first(b, peak):
            keys = every[0][b, :, :columns]
            sparse = jnp.where(row_class == classes[0][b], dot_t(picked, keys) * factor, MASKED)
            scores_sc[b] = sparse
            return jnp.maximum(peak, jnp.max(sparse, axis=1, keepdims=True))

        peak_sparse = lax.fori_loop(0, n, first, jnp.full((slots, 1), MASKED, f32))

        def second(b, carry):
            total, summed = carry
            weights = jnp.exp2(scores_sc[b] - peak_sparse)
            values = every[0][b, :, LANES : LANES + columns]
            return total + jnp.sum(weights, axis=1, keepdims=True), summed + dot(weights.astype(bf16), values)

        total_sparse, summed_sparse = lax.fori_loop(
            0, n, second, (jnp.zeros((slots, 1), f32), jnp.zeros((slots, columns), f32))
        )

    mixed = jnp.zeros((slots, columns), f32)
    for h in range(heads):
        query = jnp.where(head_of == h, q, jnp.zeros((), bf16))
        scores = dot_t(query, key_local) * factor + bias_local
        peak = jnp.max(scores, axis=1, keepdims=True)
        weights = jnp.exp2(scores - peak)
        total = jnp.sum(weights, axis=1, keepdims=True)
        summed = dot(weights.astype(bf16), value_local)
        has = row_class == (h & (RATE - 1))
        highest = jnp.where(has, jnp.maximum(peak, peak_sparse), peak)
        first_weight = jnp.exp2(peak - highest)
        second_weight = jnp.where(has, jnp.exp2(peak_sparse - highest), 0.0)
        share_of = 1.0 / (first_weight * total + second_weight * total_sparse)
        both = (first_weight * share_of) * summed + (second_weight * share_of) * summed_sparse
        mixed = jnp.where(head_of == h, both, mixed)
    att_ref[...] = jnp.where(occupied > 0.5, mixed, 0.0).T.astype(bf16)


def attend(local, every, classes, n, slots, columns):
    groups = len(local)
    tiles = every[0].shape[-2]
    stored = (n, slots, tiles) if groups == 1 and n > 1 else (1, 8, 128)
    return pl.pallas_call(
        functools.partial(attend_kernel, n, groups, columns),
        in_specs=[VMEM] * (3 * groups),
        out_specs=VMEM,
        out_shape=jax.ShapeDtypeStruct((columns, slots), bf16),
        scratch_shapes=[pltpu.VMEM(stored, f32)],
        compiler_params=pltpu.CompilerParams(vmem_limit_bytes=(24 if n <= 4 else 48) * MIB),
        cost_estimate=pl.CostEstimate(
            flops=4 * slots * columns * (4 * slots + n * tiles),
            bytes_accessed=2 * n * tiles * columns,
            transcendentals=slots * (4 * slots + n * tiles),
        ),
        name="attend",
    )(*local, *every, *classes)


def output_kernel(groups, a0, a1, a2, a3, w0, w1, w2, w3, *refs):
    residual, out_ref = refs[:groups], refs[groups]
    here = seq_index()
    total = None
    for weight, piece in ((w0, a0), (w1, a1), (w2, a2), (w3, a3)):
        part = lax.dot_general(weight[...], piece[...], (((0,), (0,)), ((), ())), preferred_element_type=f32)
        total = part if total is None else total + part
    if groups == 1:
        out_ref[...] = (total + residual[0][...].astype(f32)).astype(bf16)
    else:
        cap = residual[0].shape[1]
        for k in range(groups):
            at = pl.multiple_of((here ^ k) * cap, cap)
            block = total[:, k * cap : (k + 1) * cap] + residual[k][...].astype(f32)
            out_ref[:, pl.ds(at, cap)] = block.astype(bf16)


def project_out(attended, weights, residual):
    return pl.pallas_call(
        functools.partial(output_kernel, len(residual)),
        in_specs=[VMEM] * (8 + len(residual)),
        out_specs=VMEM,
        out_shape=jax.ShapeDtypeStruct((weights[0].shape[1], attended[0].shape[1]), bf16),
        compiler_params=pltpu.CompilerParams(vmem_limit_bytes=16 * MIB),
        name="project_out",
    )(*attended, *weights, *residual)


def per_device(
    class_rows,
    destination,
    norm1_gain,
    gate_weight,
    up_weight,
    down_weight,
    layer_scale,
    norm2_gain,
    proj_weight,
    norm3_gain,
    query_weight,
    key_weight,
    value_weight,
    out_weight,
):
    tiles = class_rows.shape[0]
    n = lax.axis_size("seq")
    me = lax.axis_index("mdl")
    columns = query_weight.shape[1]
    slots = 2 * tiles
    cap = slots // n
    few = n <= 4

    def over_mdl(value, k):
        return lax.ppermute(value, "mdl", [(i, i ^ k) for i in range(4)])

    def over_seq(value, k):
        return lax.ppermute(value, "seq", [(i, i ^ k) for i in range(n)])

    def after(value, *earlier):
        return lax.optimization_barrier((value, *earlier))[0]

    proj = proj_weight.T
    keep, send = feed_forward(class_rows, norm1_gain, gate_weight, up_weight, down_weight)
    near = over_mdl(send, 1)
    summed = (keep + near.astype(f32)).astype(bf16)
    far = over_mdl(summed, 2)
    proj_near = over_mdl(after(proj, summed), 1)
    owner = after(destination, summed).reshape(1, tiles)
    if few:
        owners = [owner] + [over_seq(owner, k) for k in range(1, n)]
    else:
        owners = [lax.all_gather(owner, "seq", axis=0)]
    embedded = embed(
        class_rows, summed, after(far, *owners), layer_scale, norm2_gain, proj, proj_near
    )

    weights = (query_weight.T, key_weight.T, value_weight.T)
    if few:
        ready, acrosses = [], []
        for k in range(n):
            own = over_seq(embedded, k) if k else embedded
            if k == 2:
                own = after(own, ready[0][0])
            across = over_mdl(own, 2)
            if k == 3:
                across = after(across, ready[1][0])
            acrosses.append(across)
            pieces = [own, over_mdl(own, 1), across, over_mdl(across, 1)]
            ready.append(prepare(pieces, owners[k], norm3_gain, weights, cap))
        out_late = after(out_weight, acrosses[0])
    else:
        sides = lax.all_gather(embedded, "mdl", axis=0).reshape(2, 2, tiles // 2, -1)
        block = sides.transpose(1, 2, 0, 3).reshape(tiles, -1)
        gathered = lax.all_gather(block, "seq", axis=0)
        ready = [prepare([gathered], owners[0], norm3_gain, weights, cap)]
        out_late = after(out_weight, embedded)

    def columns_of(value, k):
        return lax.dynamic_slice_in_dim(value, k * columns, columns, axis=1)

    paired = lax.dynamic_slice_in_dim(out_late, (me ^ 2) // 2 * (2 * columns), 2 * columns, axis=1)
    out_far = over_mdl(paired, 2)
    out_blocks = [
        columns_of(out_late, me),
        over_mdl(columns_of(out_late, me ^ 1), 1),
        columns_of(out_far, me % 2),
        over_mdl(columns_of(out_far, (me ^ 1) % 2), 1),
    ]
    local, every, classes, residual = (list(items) for items in zip(*ready))
    local, out_blocks = lax.optimization_barrier((local, out_blocks))
    attended = attend(local, every, classes, n, slots, columns)
    if not few:
        residual = [residual[0].transpose(1, 0, 2).reshape(columns, slots)]

    beyond = over_mdl(attended, 2)
    gathered = [attended, over_mdl(attended, 1), beyond, over_mdl(beyond, 1)]
    return project_out(gathered, out_blocks, residual).T


def solution(mesh):
    return jax.shard_map(
        per_device,
        mesh=mesh,
        in_specs=(
            P(("grp", "seq"), None),
            P(("grp", "seq"), None),
            P(),
            P(None, "mdl"),
            P(None, "mdl"),
            P("mdl", None),
            P(),
            P(),
            P(None, "mdl"),
            P(),
            P(None, "mdl"),
            P(None, "mdl"),
            P(None, "mdl"),
            P("mdl", None),
        ),
        out_specs=P(("grp", "seq"), "mdl"),
        check_vma=False,
    )
```

```python
import functools

import jax
import jax.numpy as jnp
from jax import lax
from jax.experimental import pallas as pl
from jax.experimental.pallas import tpu as pltpu
from jax.sharding import PartitionSpec as P

HD = 48
RATE = 4
EPSILON = 1e-06
MASKED = -1e30
MIB = 1024 * 1024
LOG2E = 1.4426950408889634

f32 = jnp.float32
bf16 = jnp.bfloat16


def layer_norm(features, norm_gain):
    middle = jnp.mean(features, axis=-1, keepdims=True)
    centred = features - middle
    spread = jnp.mean(centred * centred, axis=-1, keepdims=True)
    return centred * lax.rsqrt(spread + EPSILON) * norm_gain


def dot(a, b):
    return jnp.dot(a, b, preferred_element_type=f32)


def dot_t(a, b):
    return lax.dot_general(a, b, (((1,), (1,)), ((), ())), preferred_element_type=f32)


def whole(shape):
    return pl.BlockSpec(shape, lambda *_: (0,) * len(shape))


VMEM = pl.BlockSpec(memory_space=pltpu.VMEM)


def mdl_index():
    return lax.axis_index("mdl")


def seq_index():
    return lax.axis_index("seq")


def row(ref):
    return ref[...].reshape(1, ref.shape[0])


def ffn_kernel(
    rows_ref, gain_ref, gate_ref, up_ref, down_ref, keep_ref, send_ref,
    rows, gate, upward, down, normed, sems,
):
    me = mdl_index()
    half = keep_ref.shape[0]
    pairs = ((rows_ref, rows), (gate_ref, gate), (up_ref, upward), (down_ref, down))
    copies = [pltpu.make_async_copy(source, target, sems.at[i]) for i, (source, target) in enumerate(pairs)]
    for copy in copies:
        copy.start()
    copies[0].wait()
    for place in range(2):
        start = pl.multiple_of(((me & 1) ^ place) * half, half)
        part = rows[pl.ds(start, half), :].astype(f32)
        normed[place * half : (place + 1) * half, :] = layer_norm(part, row(gain_ref)).astype(bf16)
    copies[1].wait()
    opened = dot(normed[...], gate[...])
    opened = opened * jax.nn.sigmoid(opened)
    copies[2].wait()
    hidden = (opened * dot(normed[...], upward[...])).astype(bf16)
    keep_ref[...] = hidden[:half, :]
    copies[3].wait()
    send_ref[...] = dot(hidden[half:, :], down[...]).astype(bf16)


def feed_forward(rows, gain, gate_weight, up_weight, down_weight):
    tiles, width = rows.shape
    hidden = gate_weight.shape[1]
    half = tiles // 2
    far = pl.BlockSpec(memory_space=pltpu.HBM)
    return pl.pallas_call(
        ffn_kernel,
        in_specs=[far, VMEM, far, far, far],
        out_specs=[VMEM, VMEM],
        out_shape=[jax.ShapeDtypeStruct((half, hidden), bf16), jax.ShapeDtypeStruct((half, width), bf16)],
        scratch_shapes=[
            pltpu.VMEM((tiles, width), bf16),
            pltpu.VMEM((width, hidden), bf16),
            pltpu.VMEM((width, hidden), bf16),
            pltpu.VMEM((hidden, width), bf16),
            pltpu.VMEM((tiles, width), bf16),
            pltpu.SemaphoreType.DMA((4,)),
        ],
        compiler_params=pltpu.CompilerParams(vmem_limit_bytes=60 * MIB),
        cost_estimate=pl.CostEstimate(
            flops=6 * tiles * width * hidden, bytes_accessed=6 * width * hidden, transcendentals=tiles * hidden
        ),
        name="feed_forward",
    )(rows, gain, gate_weight, up_weight, down_weight)


def gather_kernel(hidden_ref, down_ref, near_ref, out_ref):
    out_ref[...] = (dot(hidden_ref[...], down_ref[...]) + near_ref[...].astype(f32)).astype(bf16)


def gather_sums(hidden, down_weight, near):
    return pl.pallas_call(
        gather_kernel,
        in_specs=[VMEM] * 3,
        out_specs=VMEM,
        out_shape=jax.ShapeDtypeStruct(near.shape, bf16),
        compiler_params=pltpu.CompilerParams(vmem_limit_bytes=16 * MIB),
        name="gather_sums",
    )(hidden, down_weight, near)


def embed_kernel(rows_ref, here_ref, far_ref, scale_ref, gain_ref, own, near, out_ref, blocks):
    core = mdl_index() & 1
    half = here_ref.shape[0]
    start = pl.multiple_of(core * half, half)
    rows = rows_ref[pl.ds(start, half), :].astype(f32)
    feedfwd = here_ref[...].astype(f32) + far_ref[...].astype(f32)
    stream = rows + row(scale_ref) * feedfwd
    final = layer_norm(stream, row(gain_ref)).astype(bf16)
    blocks[core] = dot_t(final, own[...])
    blocks[core ^ 1] = dot_t(final, near[...])
    out_ref[...] = jnp.concatenate([blocks[0], blocks[1]], axis=1).astype(bf16)


def embed(rows, here, far, scale, gain, own, near):
    half, width = here.shape
    columns = own.shape[0]
    return pl.pallas_call(
        embed_kernel,
        in_specs=[VMEM] * 7,
        out_specs=VMEM,
        out_shape=jax.ShapeDtypeStruct((half, 2 * columns), bf16),
        scratch_shapes=[pltpu.VMEM((2, half, columns), f32)],
        compiler_params=pltpu.CompilerParams(vmem_limit_bytes=16 * MIB),
        cost_estimate=pl.CostEstimate(
            flops=4 * half * width * columns, bytes_accessed=4 * width * columns, transcendentals=0
        ),
        name="embed",
    )(rows, here, far, scale, gain, own, near)


LANES = 256


def plan_kernel(groups, n, *refs):
    here = seq_index()
    for owner_ref, chosen_ref, bias_ref in zip(refs[:groups], refs[groups : 2 * groups], refs[2 * groups :]):
        owner = owner_ref[...]
        cap, tiles = chosen_ref.shape
        rows = lax.broadcasted_iota(jnp.int32, (tiles, tiles), 0)
        lanes = lax.broadcasted_iota(jnp.int32, (tiles, tiles), 1)
        named = lax.broadcasted_iota(jnp.int32, (max(n, 8), tiles), 0) == owner
        onehot = jnp.where(named, 1.0, 0.0)
        earlier = dot(onehot.astype(bf16), jnp.where(rows < lanes, 1.0, 0.0).astype(bf16))
        arrival = jnp.sum(onehot * earlier, axis=0, keepdims=True)
        slot = lax.broadcasted_iota(jnp.int32, (cap, tiles), 0)
        taken = (slot == arrival.astype(jnp.int32)) & (owner == here)
        chosen_ref[...] = jnp.where(taken, 1.0, 0.0).astype(bf16)
        column = jnp.sum(jnp.where(rows == lanes, arrival, 0.0), axis=1, keepdims=True).astype(jnp.int32)
        kept = lax.broadcasted_iota(jnp.int32, bias_ref.shape, 1) == (column & (RATE - 1))
        bias_ref[...] = jnp.where(kept, 0.0, MASKED).astype(bf16)


def plan(owners, n, cap, spare):
    groups = len(owners)
    tiles = owners[0].shape[-1]
    if groups > 1 or n == 1:
        count, lead, block = 1, (), whole
    else:
        count, lead = n, (n,)

        def block(shape):
            return pl.BlockSpec((None, *shape), lambda b: (b, 0, 0))

    shapes = [(cap, tiles)] * groups + [(tiles, spare)] * groups
    outs = pl.pallas_call(
        functools.partial(plan_kernel, groups, n),
        grid=(count,),
        in_specs=[block((1, tiles))] * groups,
        out_specs=[block(shape) for shape in shapes],
        out_shape=[jax.ShapeDtypeStruct(lead + shape, bf16) for shape in shapes],
        compiler_params=pltpu.CompilerParams(vmem_limit_bytes=16 * MIB),
        name="plan",
    )(*owners)
    return list(zip(outs[:groups], outs[groups:]))


def prepare_kernel(loose, *refs):
    pieces = refs[:loose]
    chosen_ref, bias_ref, gain_ref, wq, wk, wv, local_ref, all_ref, residual_ref, block = refs[loose:]
    me = mdl_index()
    tiles, width = block.shape
    columns = wq.shape[0]
    if loose > 1:
        half, side = tiles // 2, width // 2
        for km in range(4):
            at = pl.multiple_of(((me ^ km) & 1) * half, half)
            over = pl.multiple_of(((me ^ km) >> 1) * side, side)
            block[pl.ds(at, half), pl.ds(over, side)] = pieces[km][...]
        rows = block[...]
    else:
        rows = pieces[0][...]
    chosen = chosen_ref[...]
    cap = chosen.shape[0]
    mine = (
        lax.broadcasted_iota(jnp.int32, (columns, width), 1)
        == lax.broadcasted_iota(jnp.int32, (columns, width), 0) + me * columns
    )
    picked = jnp.where(mine, 1.0, 0.0).astype(bf16)
    residual_ref[...] = dot_t(dot_t(picked, rows).astype(bf16), chosen).astype(bf16)
    normed = layer_norm(rows.astype(f32), row(gain_ref)).astype(bf16)
    queries = dot_t(normed, wq[...]).astype(bf16)
    keys = dot_t(normed, wk[...]).astype(bf16)
    values = dot_t(normed, wv[...]).astype(bf16)
    occupied = jnp.sum(chosen.astype(f32), axis=1, keepdims=True)
    all_ref[:, :columns] = keys
    all_ref[:, columns:LANES] = bias_ref[...]
    all_ref[:, LANES : LANES + columns] = values
    local_ref[:, :columns] = dot(chosen, queries).astype(bf16)
    local_ref[:, columns:LANES] = jnp.zeros((cap, LANES - columns), bf16)
    local_ref[:, LANES : LANES + columns] = dot(chosen, keys).astype(bf16)
    local_ref[:, LANES + columns : 2 * LANES] = jnp.broadcast_to(
        jnp.where(occupied > 0.5, 0.0, MASKED), (cap, LANES - columns)
    ).astype(bf16)
    local_ref[:, 2 * LANES : 2 * LANES + columns] = dot(chosen, values).astype(bf16)


def prepare(pieces, planned, gain, weights):
    columns, width = weights[0].shape
    loose = len(pieces)
    chosen, bias = planned
    cap, tiles = chosen.shape[-2:]
    if loose > 1:
        count, lead, block = 1, (), whole
    else:
        count, lead = chosen.shape[0], (chosen.shape[0],)

        def block(shape):
            return pl.BlockSpec((None, *shape), lambda b: (b, 0, 0))

    first = [block(piece.shape[-2:]) for piece in pieces] + [block((cap, tiles)), block(bias.shape[-2:])]
    outs = [((cap, 3 * LANES), bf16), ((tiles, 2 * LANES), bf16), ((columns, cap), bf16)]
    return pl.pallas_call(
        functools.partial(prepare_kernel, loose),
        grid=(count,),
        in_specs=first + [whole((width,))] + [whole((columns, width))] * 3,
        out_specs=[block(shape) for shape, _ in outs],
        out_shape=[jax.ShapeDtypeStruct(lead + shape, kind) for shape, kind in outs],
        scratch_shapes=[pltpu.VMEM((tiles, width), bf16)],
        compiler_params=pltpu.CompilerParams(vmem_limit_bytes=16 * MIB),
        cost_estimate=pl.CostEstimate(
            flops=6 * count * tiles * width * columns, bytes_accessed=6 * width * columns, transcendentals=0
        ),
        name="prepare",
    )(*pieces, chosen, bias, gain, *weights)


def attend_kernel(n, groups, columns, *refs):
    local = refs[:groups]
    every = refs[groups : 2 * groups]
    residual = refs[2 * groups : 3 * groups]
    out_weight, mine_ref, pass_ref, send_ref, scores_sc, blocks = refs[3 * groups :]
    heads = columns // HD
    slots = mine_ref.shape[1]
    me, here = mdl_index(), seq_index()
    factor = HD ** (-0.5) * LOG2E
    zero, one = jnp.zeros((), bf16), jnp.ones((), bf16)

    def taken(sources, start, size):
        parts = [ref[..., start : start + size].reshape(-1, size) for ref in sources]
        return parts[0] if groups == 1 else jnp.concatenate(parts, axis=0)

    q = taken(local, 0, LANES)
    key_local = taken(local, LANES, LANES)
    value_local = taken(local, 2 * LANES, columns)
    lane = lax.broadcasted_iota(jnp.int32, (slots, LANES), 1)
    head_lane = lane // HD
    head_of = head_lane[:, :columns]
    row_class = lax.broadcasted_iota(jnp.int32, (slots, 1), 0) & (RATE - 1)
    inside = lane < columns
    class_lane = jnp.where(inside, head_lane & (RATE - 1), lane - columns)
    picked = jnp.where(class_lane == row_class, jnp.where(inside, q, one), zero)
    stored = groups == 1 and n > 1
    if not stored:
        scores_sparse = dot_t(picked, taken(every, 0, LANES)) * factor
        peak_sparse = jnp.max(scores_sparse, axis=1, keepdims=True)
    else:

        def first(b, peak):
            scores_sc[b] = dot_t(picked, every[0][b, :, :LANES]) * factor
            return jnp.maximum(peak, jnp.max(scores_sc[b], axis=1, keepdims=True))

        peak_sparse = lax.fori_loop(0, n, first, jnp.full((slots, 1), MASKED, f32))

    ones = jnp.where(lane == columns, one, zero)
    numerator = jnp.zeros((slots, columns), f32)
    denominator = jnp.zeros((slots, columns), f32)
    peak_shared = peak_sparse
    for h in range(heads):
        query = jnp.where(head_lane == h, q, ones)
        scores = dot_t(query, key_local) * factor
        peak = jnp.max(scores, axis=1, keepdims=True)
        has = row_class == (h & (RATE - 1))
        peak = jnp.where(has, jnp.maximum(peak, peak_sparse), peak)
        peak_shared = jnp.where(has, peak, peak_shared)
        weights = jnp.exp2(scores - peak)
        total = jnp.sum(weights, axis=1, keepdims=True)
        numerator = jnp.where(head_of == h, dot(weights.astype(bf16), value_local), numerator)
        denominator = jnp.where(head_of == h, total, denominator)
    if not stored:
        weights = jnp.exp2(scores_sparse - peak_shared)
        total = jnp.sum(weights, axis=1, keepdims=True)
        summed = dot(weights.astype(bf16), taken(every, LANES, columns))
    else:

        def second(b, carry):
            weights = jnp.exp2(scores_sc[b] - peak_shared)
            values = every[0][b, :, LANES : LANES + columns]
            return carry[0] + jnp.sum(weights, axis=1, keepdims=True), carry[1] + dot(weights.astype(bf16), values)

        total, summed = lax.fori_loop(
            0, n, second, (jnp.zeros((slots, 1), f32), jnp.zeros((slots, columns), f32))
        )
    own_class = (head_of & (RATE - 1)) == row_class
    numerator = numerator + jnp.where(own_class, summed, 0.0)
    denominator = denominator + jnp.where(own_class, total, 0.0)
    occupied = key_local[:, columns : columns + 1].astype(f32) > -1.0
    attended = jnp.where(occupied, numerator / denominator, 0.0).T.astype(bf16)
    partial = lax.dot_general(out_weight[...], attended, (((0,), (0,)), ((), ())), preferred_element_type=f32)
    for k in range(4):
        blocks[k] = partial[k * columns : (k + 1) * columns, :]
    if groups == 1:
        mine_ref[...] = blocks[me] + residual[0][...].astype(f32)
        pass_ref[...] = blocks[me ^ 2]
        send_ref[:columns, :] = blocks[me ^ 1].astype(bf16)
        send_ref[columns:, :] = blocks[me ^ 3].astype(bf16)
    else:
        cap = slots // groups
        for k in range(groups):
            there = pl.ds(pl.multiple_of((here ^ k) * cap, cap), cap)
            part = slice(k * cap, (k + 1) * cap)
            mine_ref[:, there] = blocks[me, :, part] + residual[k][...].astype(f32)
            pass_ref[:, there] = blocks[me ^ 2, :, part]
            send_ref[:columns, there] = blocks[me ^ 1, :, part].astype(bf16)
            send_ref[columns:, there] = blocks[me ^ 3, :, part].astype(bf16)


def attend(local, every, residual, out_weight, n, slots, columns):
    groups = len(local)
    tiles = every[0].shape[-2]
    stored = (n, slots, tiles) if groups == 1 and n > 1 else (1, 8, 128)
    return pl.pallas_call(
        functools.partial(attend_kernel, n, groups, columns),
        in_specs=[VMEM] * (3 * groups + 1),
        out_specs=[VMEM] * 3,
        out_shape=[
            jax.ShapeDtypeStruct((columns, slots), f32),
            jax.ShapeDtypeStruct((columns, slots), f32),
            jax.ShapeDtypeStruct((2 * columns, slots), bf16),
        ],
        scratch_shapes=[pltpu.VMEM(stored, f32), pltpu.VMEM((4, columns, slots), f32)],
        compiler_params=pltpu.CompilerParams(vmem_limit_bytes=(24 if n <= 4 else 48) * MIB),
        cost_estimate=pl.CostEstimate(
            flops=4 * slots * columns * (4 * slots + n * tiles),
            bytes_accessed=2 * n * tiles * columns,
            transcendentals=slots * (4 * slots + n * tiles),
        ),
        name="attend",
    )(*local, *every, *residual, out_weight)


def per_device(
    class_rows,
    destination,
    norm1_gain,
    gate_weight,
    up_weight,
    down_weight,
    layer_scale,
    norm2_gain,
    proj_weight,
    norm3_gain,
    query_weight,
    key_weight,
    value_weight,
    out_weight,
):
    tiles = class_rows.shape[0]
    n = lax.axis_size("seq")
    me = lax.axis_index("mdl")
    columns = query_weight.shape[1]
    slots = 2 * tiles
    cap = slots // n
    few = n <= 4

    def over_mdl(value, k):
        return lax.ppermute(value, "mdl", [(i, i ^ k) for i in range(4)])

    def over_seq(value, k):
        return lax.ppermute(value, "seq", [(i, i ^ k) for i in range(n)])

    def after(value, *earlier):
        return lax.optimization_barrier((value, *earlier))[0]

    proj = proj_weight.T
    keep, send = feed_forward(class_rows, norm1_gain, gate_weight, up_weight, down_weight)
    near = over_mdl(send, 1)
    summed = gather_sums(keep, down_weight, near)
    far = over_mdl(summed, 2)
    proj_near = over_mdl(after(proj, summed), 1)
    owner = after(destination, summed).reshape(1, tiles)
    if few:
        owners = [owner] + [over_seq(owner, k) for k in range(1, n)]
    else:
        owners = [lax.all_gather(owner, "seq", axis=0)]
    planned = plan(owners, n, cap, LANES - columns)
    embedded = embed(
        class_rows, summed, after(far, *owners, *planned[0]), layer_scale, norm2_gain, proj, proj_near
    )

    weights = (query_weight.T, key_weight.T, value_weight.T)
    if few:
        spare = after(embedded, embedded[:8, :128] + embedded[8:16, :128])
        owns = [spare] + [over_seq(spare if k == 1 else embedded, k) for k in range(1, n)]
        ready = []
        for k in range(n):
            own = owns[k]
            across = over_mdl(own, 2)
            if k == 3:
                across = after(across, ready[1][0])
            if k == 2:
                across = after(across, ready[0][0])
            pieces = [own, over_mdl(own, 1), across, over_mdl(across, 1)]
            ready.append(prepare(pieces, planned[k], norm3_gain, weights))
    else:
        sides = lax.all_gather(embedded, "mdl", axis=0).reshape(2, 2, tiles // 2, -1)
        block = sides.transpose(1, 2, 0, 3).reshape(tiles, -1)
        gathered = lax.all_gather(block, "seq", axis=0)
        ready = [prepare([gathered], planned[0], norm3_gain, weights)]

    local, every, residual = (list(items) for items in zip(*ready))
    if not few:
        residual = [residual[0].transpose(1, 0, 2).reshape(columns, slots)]
    mine, passing, others = attend(local, every, residual, out_weight, n, slots, columns)
    nearer = over_mdl(others, 1)
    farther = over_mdl((passing + nearer[columns:].astype(f32)).astype(bf16), 2)
    total = mine + nearer[:columns].astype(f32) + farther.astype(f32)
    return total.astype(bf16).T


def solution(mesh):
    return jax.shard_map(
        per_device,
        mesh=mesh,
        in_specs=(
            P(("grp", "seq"), None),
            P(("grp", "seq"), None),
            P(),
            P(None, "mdl"),
            P(None, "mdl"),
            P("mdl", None),
            P(),
            P(),
            P(None, "mdl"),
            P(),
            P(None, "mdl"),
            P(None, "mdl"),
            P(None, "mdl"),
            P("mdl", None),
        ),
        out_specs=P(("grp", "seq"), "mdl"),
        check_vma=False,
    )
```

```python
import functools

import jax
import jax.numpy as jnp
from jax import lax
from jax.experimental import pallas as pl
from jax.experimental.pallas import tpu as pltpu
from jax.sharding import PartitionSpec as P

HD = 48
RATE = 4
EPSILON = 1e-06
MASKED = -1e30
MIB = 1024 * 1024
LOG2E = 1.4426950408889634

f32 = jnp.float32
bf16 = jnp.bfloat16


def layer_norm(features, norm_gain):
    middle = jnp.mean(features, axis=-1, keepdims=True)
    centred = features - middle
    spread = jnp.mean(centred * centred, axis=-1, keepdims=True)
    return centred * lax.rsqrt(spread + EPSILON) * norm_gain


def dot(a, b):
    return jnp.dot(a, b, preferred_element_type=f32)


def dot_t(a, b):
    return lax.dot_general(a, b, (((1,), (1,)), ((), ())), preferred_element_type=f32)


def whole(shape):
    return pl.BlockSpec(shape, lambda *_: (0,) * len(shape))


VMEM = pl.BlockSpec(memory_space=pltpu.VMEM)


def mdl_index():
    return lax.axis_index("mdl")


def seq_index():
    return lax.axis_index("seq")


def row(ref):
    return ref[...].reshape(1, ref.shape[0])


def ffn_kernel(
    rows_ref, gain_ref, gate_ref, up_ref, down_ref, keep_ref, send_ref,
    rows, gate, upward, down, normed, sems,
):
    me = mdl_index()
    half = keep_ref.shape[0]
    pairs = ((rows_ref, rows), (gate_ref, gate), (up_ref, upward), (down_ref, down))
    copies = [pltpu.make_async_copy(source, target, sems.at[i]) for i, (source, target) in enumerate(pairs)]
    for copy in copies:
        copy.start()
    copies[0].wait()
    for place in range(2):
        start = pl.multiple_of(((me & 1) ^ place) * half, half)
        part = rows[pl.ds(start, half), :].astype(f32)
        normed[place * half : (place + 1) * half, :] = layer_norm(part, row(gain_ref)).astype(bf16)
    copies[1].wait()
    opened = dot(normed[...], gate[...])
    opened = opened * jax.nn.sigmoid(opened)
    copies[2].wait()
    hidden = (opened * dot(normed[...], upward[...])).astype(bf16)
    copies[3].wait()
    send_ref[...] = dot(hidden[half:, :], down[...]).astype(bf16)
    keep_ref[...] = dot(hidden[:half, :], down[...]).astype(bf16)


def feed_forward(rows, gain, gate_weight, up_weight, down_weight):
    tiles, width = rows.shape
    hidden = gate_weight.shape[1]
    half = tiles // 2
    far = pl.BlockSpec(memory_space=pltpu.HBM)
    return pl.pallas_call(
        ffn_kernel,
        in_specs=[far, VMEM, far, far, far],
        out_specs=[VMEM, VMEM],
        out_shape=[jax.ShapeDtypeStruct((half, width), bf16)] * 2,
        scratch_shapes=[
            pltpu.VMEM((tiles, width), bf16),
            pltpu.VMEM((width, hidden), bf16),
            pltpu.VMEM((width, hidden), bf16),
            pltpu.VMEM((hidden, width), bf16),
            pltpu.VMEM((tiles, width), bf16),
            pltpu.SemaphoreType.DMA((4,)),
        ],
        compiler_params=pltpu.CompilerParams(vmem_limit_bytes=105 * MIB // 2),
        cost_estimate=pl.CostEstimate(
            flops=6 * tiles * width * hidden, bytes_accessed=6 * width * hidden, transcendentals=tiles * hidden
        ),
        name="feed_forward",
    )(rows, gain, gate_weight, up_weight, down_weight)


def gather_kernel(keep_ref, near_ref, out_ref):
    out_ref[...] = (keep_ref[...].astype(f32) + near_ref[...].astype(f32)).astype(bf16)


def gather_sums(keep, near):
    return pl.pallas_call(
        gather_kernel,
        in_specs=[VMEM] * 2,
        out_specs=VMEM,
        out_shape=jax.ShapeDtypeStruct(near.shape, bf16),
        compiler_params=pltpu.CompilerParams(vmem_limit_bytes=16 * MIB),
        name="gather_sums",
    )(keep, near)


def embed_kernel(rows_ref, here_ref, far_ref, scale_ref, gain_ref, own, near, out_ref, blocks):
    core = mdl_index() & 1
    half = here_ref.shape[0]
    start = pl.multiple_of(core * half, half)
    rows = rows_ref[pl.ds(start, half), :].astype(f32)
    feedfwd = here_ref[...].astype(f32) + far_ref[...].astype(f32)
    stream = rows + row(scale_ref) * feedfwd
    final = layer_norm(stream, row(gain_ref)).astype(bf16)
    blocks[core] = dot_t(final, own[...])
    blocks[core ^ 1] = dot_t(final, near[...])
    out_ref[...] = jnp.concatenate([blocks[0], blocks[1]], axis=1).astype(bf16)


def embed(rows, here, far, scale, gain, own, near):
    half, width = here.shape
    columns = own.shape[0]
    return pl.pallas_call(
        embed_kernel,
        in_specs=[VMEM] * 7,
        out_specs=VMEM,
        out_shape=jax.ShapeDtypeStruct((half, 2 * columns), bf16),
        scratch_shapes=[pltpu.VMEM((2, half, columns), f32)],
        compiler_params=pltpu.CompilerParams(vmem_limit_bytes=16 * MIB),
        cost_estimate=pl.CostEstimate(
            flops=4 * half * width * columns, bytes_accessed=4 * width * columns, transcendentals=0
        ),
        name="embed",
    )(rows, here, far, scale, gain, own, near)


LANES = 256


def plan_kernel(groups, n, *refs):
    here = seq_index()
    for owner_ref, chosen_ref, bias_ref in zip(refs[:groups], refs[groups : 2 * groups], refs[2 * groups :]):
        owner = owner_ref[...]
        cap, tiles = chosen_ref.shape
        rows = lax.broadcasted_iota(jnp.int32, (tiles, tiles), 0)
        lanes = lax.broadcasted_iota(jnp.int32, (tiles, tiles), 1)
        named = lax.broadcasted_iota(jnp.int32, (max(n, 8), tiles), 0) == owner
        onehot = jnp.where(named, 1.0, 0.0)
        earlier = dot(onehot.astype(bf16), jnp.where(rows < lanes, 1.0, 0.0).astype(bf16))
        arrival = jnp.sum(onehot * earlier, axis=0, keepdims=True)
        slot = lax.broadcasted_iota(jnp.int32, (cap, tiles), 0)
        taken = (slot == arrival.astype(jnp.int32)) & (owner == here)
        chosen_ref[...] = jnp.where(taken, 1.0, 0.0).astype(bf16)
        column = jnp.sum(jnp.where(rows == lanes, arrival, 0.0), axis=1, keepdims=True).astype(jnp.int32)
        kept = lax.broadcasted_iota(jnp.int32, bias_ref.shape, 1) == (column & (RATE - 1))
        bias_ref[...] = jnp.where(kept, 0.0, MASKED).astype(bf16)


def plan(owners, n, cap, spare):
    groups = len(owners)
    tiles = owners[0].shape[-1]
    if groups > 1 or n == 1:
        count, lead, block = 1, (), whole
    else:
        count, lead = n, (n,)

        def block(shape):
            return pl.BlockSpec((None, *shape), lambda b: (b, 0, 0))

    shapes = [(cap, tiles)] * groups + [(tiles, spare)] * groups
    outs = pl.pallas_call(
        functools.partial(plan_kernel, groups, n),
        grid=(count,),
        in_specs=[block((1, tiles))] * groups,
        out_specs=[block(shape) for shape in shapes],
        out_shape=[jax.ShapeDtypeStruct(lead + shape, bf16) for shape in shapes],
        compiler_params=pltpu.CompilerParams(vmem_limit_bytes=16 * MIB),
        name="plan",
    )(*owners)
    return list(zip(outs[:groups], outs[groups:]))


def prepare_kernel(loose, *refs):
    pieces = refs[:loose]
    chosen_ref, bias_ref, gain_ref, wq, wk, wv, local_ref, all_ref, block = refs[loose:]
    me = mdl_index()
    tiles, width = block.shape
    columns = wq.shape[0]
    if loose > 1:
        half, side = tiles // 2, width // 2
        for km in range(4):
            at = pl.multiple_of(((me ^ km) & 1) * half, half)
            over = pl.multiple_of(((me ^ km) >> 1) * side, side)
            block[pl.ds(at, half), pl.ds(over, side)] = pieces[km][...]
        rows = block[...]
    else:
        rows = pieces[0][...]
    chosen = chosen_ref[...]
    cap = chosen.shape[0]
    normed = layer_norm(rows.astype(f32), row(gain_ref)).astype(bf16)
    queries = dot_t(normed, wq[...]).astype(bf16)
    keys = dot_t(normed, wk[...]).astype(bf16)
    values = dot_t(normed, wv[...]).astype(bf16)
    occupied = jnp.sum(chosen.astype(f32), axis=1, keepdims=True)
    all_ref[:, :columns] = keys
    all_ref[:, columns:LANES] = bias_ref[...]
    all_ref[:, LANES : LANES + columns] = values
    local_ref[:, :columns] = dot(chosen, queries).astype(bf16)
    local_ref[:, columns:LANES] = jnp.zeros((cap, LANES - columns), bf16)
    local_ref[:, LANES : LANES + columns] = dot(chosen, keys).astype(bf16)
    local_ref[:, LANES + columns : 2 * LANES] = jnp.broadcast_to(
        jnp.where(occupied > 0.5, 0.0, MASKED), (cap, LANES - columns)
    ).astype(bf16)
    local_ref[:, 2 * LANES : 2 * LANES + columns] = dot(chosen, values).astype(bf16)


def prepare(pieces, planned, gain, weights):
    columns, width = weights[0].shape
    loose = len(pieces)
    chosen, bias = planned
    cap, tiles = chosen.shape[-2:]
    if loose > 1:
        count, lead, block = 1, (), whole
    else:
        count, lead = chosen.shape[0], (chosen.shape[0],)

        def block(shape):
            return pl.BlockSpec((None, *shape), lambda b: (b, 0, 0))

    first = [block(piece.shape[-2:]) for piece in pieces] + [block((cap, tiles)), block(bias.shape[-2:])]
    outs = [((cap, 3 * LANES), bf16), ((tiles, 2 * LANES), bf16)]
    return pl.pallas_call(
        functools.partial(prepare_kernel, loose),
        grid=(count,),
        in_specs=first + [whole((width,))] + [whole((columns, width))] * 3,
        out_specs=[block(shape) for shape, _ in outs],
        out_shape=[jax.ShapeDtypeStruct(lead + shape, kind) for shape, kind in outs],
        scratch_shapes=[pltpu.VMEM((tiles, width), bf16)],
        compiler_params=pltpu.CompilerParams(vmem_limit_bytes=16 * MIB),
        cost_estimate=pl.CostEstimate(
            flops=6 * count * tiles * width * columns, bytes_accessed=6 * width * columns, transcendentals=0
        ),
        name="prepare",
    )(*pieces, chosen, bias, gain, *weights)


def attend_kernel(n, groups, columns, *refs):
    local = refs[:groups]
    every = refs[groups : 2 * groups]
    out_weight, mine_ref, pass_ref, send_ref, scores_sc, blocks = refs[2 * groups :]
    heads = columns // HD
    slots = mine_ref.shape[1]
    me, here = mdl_index(), seq_index()
    factor = HD ** (-0.5) * LOG2E
    zero, one = jnp.zeros((), bf16), jnp.ones((), bf16)

    def taken(sources, start, size):
        parts = [ref[..., start : start + size].reshape(-1, size) for ref in sources]
        return parts[0] if groups == 1 else jnp.concatenate(parts, axis=0)

    q = taken(local, 0, LANES)
    key_local = taken(local, LANES, LANES)
    value_local = taken(local, 2 * LANES, columns)
    lane = lax.broadcasted_iota(jnp.int32, (slots, LANES), 1)
    head_lane = lane // HD
    head_of = head_lane[:, :columns]
    row_class = lax.broadcasted_iota(jnp.int32, (slots, 1), 0) & (RATE - 1)
    inside = lane < columns
    class_lane = jnp.where(inside, head_lane & (RATE - 1), lane - columns)
    picked = jnp.where(class_lane == row_class, jnp.where(inside, q, one), zero)
    stored = groups == 1 and n > 1
    if not stored:
        scores_sparse = dot_t(picked, taken(every, 0, LANES)) * factor
        peak_sparse = jnp.max(scores_sparse, axis=1, keepdims=True)
    else:

        def first(b, peak):
            scores_sc[b] = dot_t(picked, every[0][b, :, :LANES]) * factor
            return jnp.maximum(peak, jnp.max(scores_sc[b], axis=1, keepdims=True))

        peak_sparse = lax.fori_loop(0, n, first, jnp.full((slots, 1), MASKED, f32))

    ones = jnp.where(lane == columns, one, zero)
    numerator = jnp.zeros((slots, columns), f32)
    denominator = jnp.zeros((slots, columns), f32)
    peak_shared = peak_sparse
    for h in range(heads):
        query = jnp.where(head_lane == h, q, ones)
        scores = dot_t(query, key_local) * factor
        peak = jnp.max(scores, axis=1, keepdims=True)
        has = row_class == (h & (RATE - 1))
        peak = jnp.where(has, jnp.maximum(peak, peak_sparse), peak)
        peak_shared = jnp.where(has, peak, peak_shared)
        weights = jnp.exp2(scores - peak)
        total = jnp.sum(weights, axis=1, keepdims=True)
        numerator = jnp.where(head_of == h, dot(weights.astype(bf16), value_local), numerator)
        denominator = jnp.where(head_of == h, total, denominator)
    if not stored:
        weights = jnp.exp2(scores_sparse - peak_shared)
        total = jnp.sum(weights, axis=1, keepdims=True)
        summed = dot(weights.astype(bf16), taken(every, LANES, columns))
    else:

        def second(b, carry):
            weights = jnp.exp2(scores_sc[b] - peak_shared)
            values = every[0][b, :, LANES : LANES + columns]
            return carry[0] + jnp.sum(weights, axis=1, keepdims=True), carry[1] + dot(weights.astype(bf16), values)

        total, summed = lax.fori_loop(
            0, n, second, (jnp.zeros((slots, 1), f32), jnp.zeros((slots, columns), f32))
        )
    own_class = (head_of & (RATE - 1)) == row_class
    numerator = numerator + jnp.where(own_class, summed, 0.0)
    denominator = denominator + jnp.where(own_class, total, 0.0)
    occupied = key_local[:, columns : columns + 1].astype(f32) > -1.0
    attended = jnp.where(occupied, numerator / denominator, 0.0).T.astype(bf16)
    partial = lax.dot_general(out_weight[...], attended, (((0,), (0,)), ((), ())), preferred_element_type=f32)
    for k in range(4):
        blocks[k] = partial[k * columns : (k + 1) * columns, :]
    if groups == 1:
        mine_ref[...] = blocks[me]
        pass_ref[...] = blocks[me ^ 2]
        send_ref[:columns, :] = blocks[me ^ 1].astype(bf16)
        send_ref[columns:, :] = blocks[me ^ 3].astype(bf16)
    else:
        cap = slots // groups
        for k in range(groups):
            there = pl.ds(pl.multiple_of((here ^ k) * cap, cap), cap)
            part = slice(k * cap, (k + 1) * cap)
            mine_ref[:, there] = blocks[me, :, part]
            pass_ref[:, there] = blocks[me ^ 2, :, part]
            send_ref[:columns, there] = blocks[me ^ 1, :, part].astype(bf16)
            send_ref[columns:, there] = blocks[me ^ 3, :, part].astype(bf16)


def attend(local, every, out_weight, n, slots, columns):
    groups = len(local)
    tiles = every[0].shape[-2]
    stored = (n, slots, tiles) if groups == 1 and n > 1 else (1, 8, 128)
    return pl.pallas_call(
        functools.partial(attend_kernel, n, groups, columns),
        in_specs=[VMEM] * (2 * groups + 1),
        out_specs=[VMEM] * 3,
        out_shape=[
            jax.ShapeDtypeStruct((columns, slots), f32),
            jax.ShapeDtypeStruct((columns, slots), f32),
            jax.ShapeDtypeStruct((2 * columns, slots), bf16),
        ],
        scratch_shapes=[pltpu.VMEM(stored, f32), pltpu.VMEM((4, columns, slots), f32)],
        compiler_params=pltpu.CompilerParams(vmem_limit_bytes=(24 if n <= 4 else 48) * MIB),
        cost_estimate=pl.CostEstimate(
            flops=4 * slots * columns * (4 * slots + n * tiles),
            bytes_accessed=2 * n * tiles * columns,
            transcendentals=slots * (4 * slots + n * tiles),
        ),
        name="attend",
    )(*local, *every, out_weight)


def residual_kernel(groups, loose, *refs):
    me, here = mdl_index(), seq_index()
    out_ref = refs[-1]
    columns = out_ref.shape[-2]
    for k in range(groups):
        chosen = refs[k][...]
        cap, tiles = chosen.shape
        pieces = refs[groups + k * loose : groups + (k + 1) * loose]
        width = pieces[0].shape[-1]
        shift = (me if loose == 1 else me & 1) * columns
        mine = (
            lax.broadcasted_iota(jnp.int32, (columns, width), 1)
            == lax.broadcasted_iota(jnp.int32, (columns, width), 0) + shift
        )
        picked = jnp.where(mine, 1.0, 0.0).astype(bf16)
        total = None
        for j, piece in enumerate(pieces):
            taken = chosen
            if loose > 1:
                half = tiles // 2
                first = (me & 1) == j
                taken = jnp.where(first, chosen[:, :half], chosen[:, half:])
            part = dot_t(dot_t(picked, piece[...]).astype(bf16), taken)
            total = part if total is None else total + part
        if loose == 1:
            out_ref[...] = total
        else:
            out_ref[:, pl.ds(pl.multiple_of((here ^ k) * cap, cap), cap)] = total


def residual_of(chosen, pieces, columns):
    groups, loose = len(chosen), len(pieces[0])
    cap = chosen[0].shape[-2]
    if loose > 1:
        count, out, block = 1, (columns, groups * cap), whole
    else:
        count, out = chosen[0].shape[0], (columns, cap)

        def block(shape):
            return pl.BlockSpec((None, *shape), lambda b: (b, 0, 0))

    args = [*chosen, *(piece for group in pieces for piece in group)]
    return pl.pallas_call(
        functools.partial(residual_kernel, groups, loose),
        grid=(count,),
        in_specs=[block(arg.shape[-2:]) for arg in args],
        out_specs=block(out),
        out_shape=jax.ShapeDtypeStruct(out if loose > 1 else (count, *out), f32),
        compiler_params=pltpu.CompilerParams(vmem_limit_bytes=16 * MIB),
        name="residual",
    )(*args)


def per_device(
    class_rows,
    destination,
    norm1_gain,
    gate_weight,
    up_weight,
    down_weight,
    layer_scale,
    norm2_gain,
    proj_weight,
    norm3_gain,
    query_weight,
    key_weight,
    value_weight,
    out_weight,
):
    tiles = class_rows.shape[0]
    n = lax.axis_size("seq")
    me = lax.axis_index("mdl")
    columns = query_weight.shape[1]
    slots = 2 * tiles
    cap = slots // n
    few = n <= 4

    def over_mdl(value, k):
        return lax.ppermute(value, "mdl", [(i, i ^ k) for i in range(4)])

    def over_seq(value, k):
        return lax.ppermute(value, "seq", [(i, i ^ k) for i in range(n)])

    def after(value, *earlier):
        return lax.optimization_barrier((value, *earlier))[0]

    proj = proj_weight.T
    keep, send = feed_forward(class_rows, norm1_gain, gate_weight, up_weight, down_weight)
    near = over_mdl(send, 1)
    summed = gather_sums(keep, near)
    far = over_mdl(summed, 2)
    proj_near = over_mdl(proj, 1)
    owner = after(destination, summed).reshape(1, tiles)
    if few:
        owners = [owner] + [over_seq(owner, k) for k in range(1, n)]
    else:
        owners = [lax.all_gather(owner, "seq", axis=0)]
    planned = plan(owners, n, cap, LANES - columns)
    embedded = embed(
        class_rows, summed, after(far, *owners, *planned[0]), layer_scale, norm2_gain, proj, proj_near
    )

    weights = (query_weight.T, key_weight.T, value_weight.T)
    if few:
        spare = after(embedded, embedded[:8, :128] + embedded[8:16, :128])
        owns = [spare] + [over_seq(spare if k == 1 else embedded, k) for k in range(1, n)]
        ready, kept = [], []
        for k in range(n):
            own = owns[k]
            across = over_mdl(own, 2)
            if k == 3:
                across = after(across, ready[1][0])
            if k == 2:
                across = after(across, ready[0][0])
            pieces = [own, over_mdl(own, 1), across, over_mdl(across, 1)]
            kept.append(pieces[:2])
            ready.append(prepare(pieces, planned[k], norm3_gain, weights))
    else:
        sides = lax.all_gather(embedded, "mdl", axis=0).reshape(2, 2, tiles // 2, -1)
        block = sides.transpose(1, 2, 0, 3).reshape(tiles, -1)
        gathered = lax.all_gather(block, "seq", axis=0)
        ready = [prepare([gathered], planned[0], norm3_gain, weights)]
        kept = [[gathered]]

    local, every = (list(items) for items in zip(*ready))
    mine, passing, others = attend(local, every, out_weight, n, slots, columns)
    chosen = [after(item[0], mine) for item in planned]
    residual = residual_of(chosen, kept, columns)
    if not few:
        residual = residual.transpose(1, 0, 2).reshape(columns, slots)
    nearer = over_mdl(others, 1)
    farther = over_mdl((passing + nearer[columns:].astype(f32)).astype(bf16), 2)
    total = mine + residual + nearer[:columns].astype(f32) + farther.astype(f32)
    return total.astype(bf16).T


def solution(mesh):
    return jax.shard_map(
        per_device,
        mesh=mesh,
        in_specs=(
            P(("grp", "seq"), None),
            P(("grp", "seq"), None),
            P(),
            P(None, "mdl"),
            P(None, "mdl"),
            P("mdl", None),
            P(),
            P(),
            P(None, "mdl"),
            P(),
            P(None, "mdl"),
            P(None, "mdl"),
            P(None, "mdl"),
            P("mdl", None),
        ),
        out_specs=P(("grp", "seq"), "mdl"),
        check_vma=False,
    )
```

```python
import functools

import jax
import jax.numpy as jnp
from jax import lax
from jax.experimental import pallas as pl
from jax.experimental.pallas import tpu as pltpu
from jax.sharding import PartitionSpec as P

HD = 48
RATE = 4
EPSILON = 1e-06
MASKED = -1e30
MIB = 1024 * 1024
LOG2E = 1.4426950408889634

f32 = jnp.float32
bf16 = jnp.bfloat16


def layer_norm(features, norm_gain):
    middle = jnp.mean(features, axis=-1, keepdims=True)
    centred = features - middle
    spread = jnp.mean(centred * centred, axis=-1, keepdims=True)
    return centred * lax.rsqrt(spread + EPSILON) * norm_gain


def dot(a, b):
    return jnp.dot(a, b, preferred_element_type=f32)


def dot_t(a, b):
    return lax.dot_general(a, b, (((1,), (1,)), ((), ())), preferred_element_type=f32)


def whole(shape):
    return pl.BlockSpec(shape, lambda *_: (0,) * len(shape))


VMEM = pl.BlockSpec(memory_space=pltpu.VMEM)


def mdl_index():
    return lax.axis_index("mdl")


def seq_index():
    return lax.axis_index("seq")


def row(ref):
    return ref[...].reshape(1, ref.shape[0])


def ffn_kernel(
    rows_ref, gain_ref, gate_ref, up_ref, down_ref, keep_ref, send_ref,
    rows, gate, upward, down, normed, sems,
):
    me = mdl_index()
    half = keep_ref.shape[0]
    pairs = ((rows_ref, rows), (gate_ref, gate), (up_ref, upward), (down_ref, down))
    copies = [pltpu.make_async_copy(source, target, sems.at[i]) for i, (source, target) in enumerate(pairs)]
    for copy in copies:
        copy.start()
    copies[0].wait()
    for place in range(2):
        start = pl.multiple_of(((me & 1) ^ place) * half, half)
        part = rows[pl.ds(start, half), :].astype(f32)
        normed[place * half : (place + 1) * half, :] = layer_norm(part, row(gain_ref)).astype(bf16)
    copies[1].wait()
    opened = dot(normed[...], gate[...])
    opened = opened * jax.nn.sigmoid(opened)
    copies[2].wait()
    hidden = (opened * dot(normed[...], upward[...])).astype(bf16)
    copies[3].wait()
    send_ref[...] = dot(hidden[half:, :], down[...]).astype(bf16)
    keep_ref[...] = dot(hidden[:half, :], down[...]).astype(bf16)


def feed_forward(rows, gain, gate_weight, up_weight, down_weight):
    tiles, width = rows.shape
    hidden = gate_weight.shape[1]
    half = tiles // 2
    far = pl.BlockSpec(memory_space=pltpu.HBM)
    return pl.pallas_call(
        ffn_kernel,
        in_specs=[far, VMEM, far, far, far],
        out_specs=[VMEM, VMEM],
        out_shape=[jax.ShapeDtypeStruct((half, width), bf16)] * 2,
        scratch_shapes=[
            pltpu.VMEM((tiles, width), bf16),
            pltpu.VMEM((width, hidden), bf16),
            pltpu.VMEM((width, hidden), bf16),
            pltpu.VMEM((hidden, width), bf16),
            pltpu.VMEM((tiles, width), bf16),
            pltpu.SemaphoreType.DMA((4,)),
        ],
        compiler_params=pltpu.CompilerParams(vmem_limit_bytes=105 * MIB // 2),
        cost_estimate=pl.CostEstimate(
            flops=6 * tiles * width * hidden, bytes_accessed=6 * width * hidden, transcendentals=tiles * hidden
        ),
        name="feed_forward",
    )(rows, gain, gate_weight, up_weight, down_weight)


def gather_kernel(keep_ref, near_ref, out_ref):
    out_ref[...] = (keep_ref[...].astype(f32) + near_ref[...].astype(f32)).astype(bf16)


def gather_sums(keep, near):
    return pl.pallas_call(
        gather_kernel,
        in_specs=[VMEM] * 2,
        out_specs=VMEM,
        out_shape=jax.ShapeDtypeStruct(near.shape, bf16),
        compiler_params=pltpu.CompilerParams(vmem_limit_bytes=16 * MIB),
        name="gather_sums",
    )(keep, near)


def embed_kernel(rows_ref, here_ref, far_ref, scale_ref, gain_ref, own, near, out_ref, blocks):
    core = mdl_index() & 1
    half = here_ref.shape[0]
    start = pl.multiple_of(core * half, half)
    rows = rows_ref[pl.ds(start, half), :].astype(f32)
    feedfwd = here_ref[...].astype(f32) + far_ref[...].astype(f32)
    stream = rows + row(scale_ref) * feedfwd
    final = layer_norm(stream, row(gain_ref)).astype(bf16)
    blocks[core] = dot_t(final, own[...])
    blocks[core ^ 1] = dot_t(final, near[...])
    out_ref[...] = jnp.concatenate([blocks[0], blocks[1]], axis=1).astype(bf16)


def embed(rows, here, far, scale, gain, own, near):
    half, width = here.shape
    columns = own.shape[0]
    return pl.pallas_call(
        embed_kernel,
        in_specs=[VMEM] * 7,
        out_specs=VMEM,
        out_shape=jax.ShapeDtypeStruct((half, 2 * columns), bf16),
        scratch_shapes=[pltpu.VMEM((2, half, columns), f32)],
        compiler_params=pltpu.CompilerParams(vmem_limit_bytes=16 * MIB),
        cost_estimate=pl.CostEstimate(
            flops=4 * half * width * columns, bytes_accessed=4 * width * columns, transcendentals=0
        ),
        name="embed",
    )(rows, here, far, scale, gain, own, near)


LANES = 256


def plan_kernel(groups, n, *refs):
    here = seq_index()
    for owner_ref, chosen_ref, bias_ref in zip(refs[:groups], refs[groups : 2 * groups], refs[2 * groups :]):
        owner = owner_ref[...]
        cap, tiles = chosen_ref.shape
        rows = lax.broadcasted_iota(jnp.int32, (tiles, tiles), 0)
        lanes = lax.broadcasted_iota(jnp.int32, (tiles, tiles), 1)
        named = lax.broadcasted_iota(jnp.int32, (max(n, 8), tiles), 0) == owner
        onehot = jnp.where(named, 1.0, 0.0)
        earlier = dot(onehot.astype(bf16), jnp.where(rows < lanes, 1.0, 0.0).astype(bf16))
        arrival = jnp.sum(onehot * earlier, axis=0, keepdims=True)
        slot = lax.broadcasted_iota(jnp.int32, (cap, tiles), 0)
        taken = (slot == arrival.astype(jnp.int32)) & (owner == here)
        chosen_ref[...] = jnp.where(taken, 1.0, 0.0).astype(bf16)
        column = jnp.sum(jnp.where(rows == lanes, arrival, 0.0), axis=1, keepdims=True).astype(jnp.int32)
        kept = lax.broadcasted_iota(jnp.int32, bias_ref.shape, 1) == (column & (RATE - 1))
        bias_ref[...] = jnp.where(kept, 0.0, MASKED).astype(bf16)


def plan(owners, n, cap, spare):
    groups = len(owners)
    tiles = owners[0].shape[-1]
    if groups > 1 or n == 1:
        count, lead, block = 1, (), whole
    else:
        count, lead = n, (n,)

        def block(shape):
            return pl.BlockSpec((None, *shape), lambda b: (b, 0, 0))

    shapes = [(cap, tiles)] * groups + [(tiles, spare)] * groups
    outs = pl.pallas_call(
        functools.partial(plan_kernel, groups, n),
        grid=(count,),
        in_specs=[block((1, tiles))] * groups,
        out_specs=[block(shape) for shape in shapes],
        out_shape=[jax.ShapeDtypeStruct(lead + shape, bf16) for shape in shapes],
        compiler_params=pltpu.CompilerParams(vmem_limit_bytes=16 * MIB),
        name="plan",
    )(*owners)
    return list(zip(outs[:groups], outs[groups:]))


def prepare_kernel(loose, *refs):
    pieces = refs[:loose]
    chosen_ref, bias_ref, gain_ref, wq, wk, wv, local_ref, all_ref, block = refs[loose:]
    me = mdl_index()
    tiles, width = block.shape
    columns = wq.shape[0]
    if loose > 1:
        half, side = tiles // 2, width // 2
        for km in range(4):
            at = pl.multiple_of(((me ^ km) & 1) * half, half)
            over = pl.multiple_of(((me ^ km) >> 1) * side, side)
            block[pl.ds(at, half), pl.ds(over, side)] = pieces[km][...]
        rows = block[...]
    else:
        rows = pieces[0][...]
    chosen = chosen_ref[...]
    cap = chosen.shape[0]
    normed = layer_norm(rows.astype(f32), row(gain_ref)).astype(bf16)
    queries = (dot_t(normed, wq[...]) * (HD ** (-0.5) * LOG2E)).astype(bf16)
    keys = dot_t(normed, wk[...]).astype(bf16)
    values = dot_t(normed, wv[...]).astype(bf16)
    occupied = jnp.sum(chosen.astype(f32), axis=1, keepdims=True)
    all_ref[:, :columns] = keys
    all_ref[:, columns:LANES] = bias_ref[...]
    all_ref[:, LANES : LANES + columns] = values
    all_ref[:, LANES + columns :] = jnp.ones((tiles, LANES - columns), bf16)
    local_ref[:, :columns] = dot(chosen, queries).astype(bf16)
    local_ref[:, columns:LANES] = jnp.zeros((cap, LANES - columns), bf16)
    local_ref[:, LANES : LANES + columns] = dot(chosen, keys).astype(bf16)
    local_ref[:, LANES + columns : 2 * LANES] = jnp.broadcast_to(
        jnp.where(occupied > 0.5, 0.0, MASKED), (cap, LANES - columns)
    ).astype(bf16)
    local_ref[:, 2 * LANES : 2 * LANES + columns] = dot(chosen, values).astype(bf16)
    local_ref[:, 2 * LANES + columns :] = jnp.ones((cap, LANES - columns), bf16)


def prepare(pieces, planned, gain, weights):
    columns, width = weights[0].shape
    loose = len(pieces)
    chosen, bias = planned
    cap, tiles = chosen.shape[-2:]
    if loose > 1:
        count, lead, block = 1, (), whole
    else:
        count, lead = chosen.shape[0], (chosen.shape[0],)

        def block(shape):
            return pl.BlockSpec((None, *shape), lambda b: (b, 0, 0))

    first = [block(piece.shape[-2:]) for piece in pieces] + [block((cap, tiles)), block(bias.shape[-2:])]
    outs = [((cap, 3 * LANES), bf16), ((tiles, 2 * LANES), bf16)]
    return pl.pallas_call(
        functools.partial(prepare_kernel, loose),
        grid=(count,),
        in_specs=first + [whole((width,))] + [whole((columns, width))] * 3,
        out_specs=[block(shape) for shape, _ in outs],
        out_shape=[jax.ShapeDtypeStruct(lead + shape, kind) for shape, kind in outs],
        scratch_shapes=[pltpu.VMEM((tiles, width), bf16)],
        compiler_params=pltpu.CompilerParams(vmem_limit_bytes=16 * MIB),
        cost_estimate=pl.CostEstimate(
            flops=6 * count * tiles * width * columns, bytes_accessed=6 * width * columns, transcendentals=0
        ),
        name="prepare",
    )(*pieces, chosen, bias, gain, *weights)


def attend_kernel(n, groups, columns, *refs):
    local = refs[:groups]
    every = refs[groups : 2 * groups]
    out_weight, mine_ref, pass_ref, send_ref, scores_sc, blocks = refs[2 * groups :]
    heads = columns // HD
    slots = mine_ref.shape[1]
    me, here = mdl_index(), seq_index()
    zero, one = jnp.zeros((), bf16), jnp.ones((), bf16)

    def taken(sources, start, size):
        parts = [ref[..., start : start + size].reshape(-1, size) for ref in sources]
        return parts[0] if groups == 1 else jnp.concatenate(parts, axis=0)

    q = taken(local, 0, LANES)
    key_local = taken(local, LANES, LANES)
    value_local = taken(local, 2 * LANES, LANES)
    lane = lax.broadcasted_iota(jnp.int32, (slots, LANES), 1)
    head_lane = lane // HD
    head_of = head_lane[:, :columns]
    row_class = lax.broadcasted_iota(jnp.int32, (slots, 1), 0) & (RATE - 1)
    inside = lane < columns
    class_lane = jnp.where(inside, head_lane & (RATE - 1), lane - columns)
    picked = jnp.where(class_lane == row_class, jnp.where(inside, q, one), zero)
    stored = groups == 1 and n > 1
    if not stored:
        scores_sparse = dot_t(picked, taken(every, 0, LANES))
        peak_sparse = jnp.max(scores_sparse, axis=1, keepdims=True)
    else:

        def first(b, peak):
            scores_sc[b] = dot_t(picked, every[0][b, :, :LANES])
            return jnp.maximum(peak, jnp.max(scores_sc[b], axis=1, keepdims=True))

        peak_sparse = lax.fori_loop(0, n, first, jnp.full((slots, 1), MASKED, f32))

    ones = jnp.where(lane == columns, one, zero)
    numerator = jnp.zeros((slots, columns), f32)
    denominator = jnp.zeros((slots, columns), f32)
    peak_shared = peak_sparse
    for h in range(heads):
        query = jnp.where(head_lane == h, q, ones)
        scores = dot_t(query, key_local)
        peak = jnp.max(scores, axis=1, keepdims=True)
        has = row_class == (h & (RATE - 1))
        peak = jnp.where(has, jnp.maximum(peak, peak_sparse), peak)
        peak_shared = jnp.where(has, peak, peak_shared)
        weights = jnp.exp2(scores - peak)
        summed = dot(weights.astype(bf16), value_local)
        numerator = jnp.where(head_of == h, summed[:, :columns], numerator)
        denominator = jnp.where(head_of == h, summed[:, columns : columns + 1], denominator)
    if not stored:
        weights = jnp.exp2(scores_sparse - peak_shared)
        summed = dot(weights.astype(bf16), taken(every, LANES, LANES))
    else:

        def second(b, carry):
            weights = jnp.exp2(scores_sc[b] - peak_shared)
            return carry + dot(weights.astype(bf16), every[0][b, :, LANES:])

        summed = lax.fori_loop(0, n, second, jnp.zeros((slots, LANES), f32))
    own_class = (head_of & (RATE - 1)) == row_class
    numerator = numerator + jnp.where(own_class, summed[:, :columns], 0.0)
    denominator = denominator + jnp.where(own_class, summed[:, columns : columns + 1], 0.0)
    occupied = key_local[:, columns : columns + 1].astype(f32) > -1.0
    attended = jnp.where(occupied, numerator / denominator, 0.0).T.astype(bf16)
    partial = lax.dot_general(out_weight[...], attended, (((0,), (0,)), ((), ())), preferred_element_type=f32)
    for k in range(4):
        blocks[k] = partial[k * columns : (k + 1) * columns, :]
    if groups == 1:
        mine_ref[...] = blocks[me]
        pass_ref[...] = blocks[me ^ 2]
        send_ref[:columns, :] = blocks[me ^ 1].astype(bf16)
        send_ref[columns:, :] = blocks[me ^ 3].astype(bf16)
    else:
        cap = slots // groups
        for k in range(groups):
            there = pl.ds(pl.multiple_of((here ^ k) * cap, cap), cap)
            part = slice(k * cap, (k + 1) * cap)
            mine_ref[:, there] = blocks[me, :, part]
            pass_ref[:, there] = blocks[me ^ 2, :, part]
            send_ref[:columns, there] = blocks[me ^ 1, :, part].astype(bf16)
            send_ref[columns:, there] = blocks[me ^ 3, :, part].astype(bf16)


def attend(local, every, out_weight, n, slots, columns):
    groups = len(local)
    tiles = every[0].shape[-2]
    stored = (n, slots, tiles) if groups == 1 and n > 1 else (1, 8, 128)
    return pl.pallas_call(
        functools.partial(attend_kernel, n, groups, columns),
        in_specs=[VMEM] * (2 * groups + 1),
        out_specs=[VMEM] * 3,
        out_shape=[
            jax.ShapeDtypeStruct((columns, slots), f32),
            jax.ShapeDtypeStruct((columns, slots), f32),
            jax.ShapeDtypeStruct((2 * columns, slots), bf16),
        ],
        scratch_shapes=[pltpu.VMEM(stored, f32), pltpu.VMEM((4, columns, slots), f32)],
        compiler_params=pltpu.CompilerParams(vmem_limit_bytes=(24 if n <= 4 else 48) * MIB),
        cost_estimate=pl.CostEstimate(
            flops=4 * slots * columns * (4 * slots + n * tiles),
            bytes_accessed=2 * n * tiles * columns,
            transcendentals=slots * (4 * slots + n * tiles),
        ),
        name="attend",
    )(*local, *every, out_weight)


def residual_kernel(groups, loose, *refs):
    me, here = mdl_index(), seq_index()
    out_ref = refs[-1]
    columns = out_ref.shape[-2]
    for k in range(groups):
        chosen = refs[k][...]
        cap, tiles = chosen.shape
        pieces = refs[groups + k * loose : groups + (k + 1) * loose]
        width = pieces[0].shape[-1]
        shift = (me if loose == 1 else me & 1) * columns
        mine = (
            lax.broadcasted_iota(jnp.int32, (columns, width), 1)
            == lax.broadcasted_iota(jnp.int32, (columns, width), 0) + shift
        )
        picked = jnp.where(mine, 1.0, 0.0).astype(bf16)
        total = None
        for j, piece in enumerate(pieces):
            taken = chosen
            if loose > 1:
                half = tiles // 2
                first = (me & 1) == j
                taken = jnp.where(first, chosen[:, :half], chosen[:, half:])
            part = dot_t(dot_t(picked, piece[...]).astype(bf16), taken)
            total = part if total is None else total + part
        if loose == 1:
            out_ref[...] = total
        else:
            out_ref[:, pl.ds(pl.multiple_of((here ^ k) * cap, cap), cap)] = total


def residual_of(chosen, pieces, columns):
    groups, loose = len(chosen), len(pieces[0])
    cap = chosen[0].shape[-2]
    if loose > 1:
        count, out, block = 1, (columns, groups * cap), whole
    else:
        count, out = chosen[0].shape[0], (columns, cap)

        def block(shape):
            return pl.BlockSpec((None, *shape), lambda b: (b, 0, 0))

    args = [*chosen, *(piece for group in pieces for piece in group)]
    return pl.pallas_call(
        functools.partial(residual_kernel, groups, loose),
        grid=(count,),
        in_specs=[block(arg.shape[-2:]) for arg in args],
        out_specs=block(out),
        out_shape=jax.ShapeDtypeStruct(out if loose > 1 else (count, *out), f32),
        compiler_params=pltpu.CompilerParams(vmem_limit_bytes=16 * MIB),
        name="residual",
    )(*args)


def per_device(
    class_rows,
    destination,
    norm1_gain,
    gate_weight,
    up_weight,
    down_weight,
    layer_scale,
    norm2_gain,
    proj_weight,
    norm3_gain,
    query_weight,
    key_weight,
    value_weight,
    out_weight,
):
    tiles = class_rows.shape[0]
    n = lax.axis_size("seq")
    me = lax.axis_index("mdl")
    columns = query_weight.shape[1]
    slots = 2 * tiles
    cap = slots // n
    few = n <= 4

    def over_mdl(value, k):
        return lax.ppermute(value, "mdl", [(i, i ^ k) for i in range(4)])

    def over_seq(value, k):
        return lax.ppermute(value, "seq", [(i, i ^ k) for i in range(n)])

    def after(value, *earlier):
        return lax.optimization_barrier((value, *earlier))[0]

    proj = proj_weight.T
    keep, send = feed_forward(class_rows, norm1_gain, gate_weight, up_weight, down_weight)
    near = over_mdl(send, 1)
    summed = gather_sums(keep, near)
    far = over_mdl(summed, 2)
    proj_near = over_mdl(proj, 1)
    owner = after(destination, summed).reshape(1, tiles)
    if few:
        owners = [owner] + [over_seq(owner, k) for k in range(1, n)]
    else:
        owners = [lax.all_gather(owner, "seq", axis=0)]
    planned = plan(owners, n, cap, LANES - columns)
    embedded = embed(
        class_rows, summed, after(far, *owners, *planned[0]), layer_scale, norm2_gain, proj, proj_near
    )

    weights = (query_weight.T, key_weight.T, value_weight.T)
    if few:
        spare = after(embedded, embedded[:8, :128] + embedded[8:16, :128])
        owns = [spare] + [over_seq(spare if k == 1 else embedded, k) for k in range(1, n)]
        ready, kept = [], []
        for k in range(n):
            own = owns[k]
            across = over_mdl(own, 2)
            if k == 3:
                across = after(across, ready[1][0])
            if k == 2:
                across = after(across, ready[0][0])
            pieces = [own, over_mdl(own, 1), across, over_mdl(across, 1)]
            kept.append(pieces[:2])
            ready.append(prepare(pieces, planned[k], norm3_gain, weights))
    else:
        sides = lax.all_gather(embedded, "mdl", axis=0).reshape(2, 2, tiles // 2, -1)
        block = sides.transpose(1, 2, 0, 3).reshape(tiles, -1)
        gathered = lax.all_gather(block, "seq", axis=0)
        ready = [prepare([gathered], planned[0], norm3_gain, weights)]
        kept = [[gathered]]

    local, every = (list(items) for items in zip(*ready))
    mine, passing, others = attend(local, every, out_weight, n, slots, columns)
    chosen = [after(item[0], mine) for item in planned]
    residual = residual_of(chosen, kept, columns)
    if not few:
        residual = residual.transpose(1, 0, 2).reshape(columns, slots)
    nearer = over_mdl(others, 1)
    farther = over_mdl((passing + nearer[columns:].astype(f32)).astype(bf16), 2)
    total = mine + residual + nearer[:columns].astype(f32) + farther.astype(f32)
    return total.astype(bf16).T


def solution(mesh):
    return jax.shard_map(
        per_device,
        mesh=mesh,
        in_specs=(
            P(("grp", "seq"), None),
            P(("grp", "seq"), None),
            P(),
            P(None, "mdl"),
            P(None, "mdl"),
            P("mdl", None),
            P(),
            P(),
            P(None, "mdl"),
            P(),
            P(None, "mdl"),
            P(None, "mdl"),
            P(None, "mdl"),
            P("mdl", None),
        ),
        out_specs=P(("grp", "seq"), "mdl"),
        check_vma=False,
    )
```
